256 devices in a mesh: grp: 16 (over y_hi, z), head: 16 (over x, y_lo, core).
Axes of the slice: x: 4, y: 4 (y_hi: 2, y_lo: 2; y = y_hi * 2 + y_lo), z: 8, core: 2. Of those that a mesh axis runs over, the one named last changes fastest.
Arguments:
- q_latent: bfloat16 [1024, 1536], P(('grp', 'head')), may hold values from -6 to 6
- draft_latent: bfloat16 [1024, 512], P(('grp', 'head')), may hold values from -6 to 6
- draft_rope: bfloat16 [1024, 64], P(('grp', 'head')), may hold values from -6 to 6
- draft_start: int32 [128], P('grp'), may hold values from 0 to 7
- prompt_latent: bfloat16 [8192, 512], P(('grp', 'head')), may hold values from -100 to 100
- prompt_rope: bfloat16 [8192, 64], P(('grp', 'head')), may hold values from -6 to 6
- w_uq: bfloat16 [1536, 24576], P(None, 'head'), may hold values from -0.15625 to 0.15625
- w_uk: bfloat16 [128, 128, 512], P('head'), may hold values from -0.5 to 0.5
- w_uv: bfloat16 [128, 512, 128], P('head'), may hold values from -0.25 to 0.25
Outputs:
- attn_out: bfloat16 [1024, 16384], P('grp', 'head')
The draws below stay inside these ranges and needn't reach their ends.
All inputs are finite; a program needn't handle non-finite values.
Results may differ from the reference program's by a relative error of at most 0.01.
The reference program's roundings to bfloat16 on the way count: a program that leaves them out, or rounds other values in their place, can miss the bound.
Values may be sent and summed in bfloat16 or wider, within the bound.
A program may use at most 64 MiB of HBM per device.

```python
import jax
import jax.numpy as jnp
from jax import lax

QLORA = 1536
KVL = 512
ROPE = 64
NOPE = 128
VD = 128
DRAFT = 8
SAMPLES_GRP = 8
PROMPT = 8192
HEADS = 128
ROWS = 1024
N_GRP = 16


def draw_prompt_latent(key, part):
    key = jax.random.fold_in(key, 7)
    base_key = jax.random.fold_in(key, 0)
    values = jax.random.normal(base_key, (PROMPT, KVL), jnp.float32)
    return jnp.clip(values, -100.0, 100.0).astype(jnp.bfloat16)


def set_ends(values, stream_key, smallest, top_value):
    spot = [jax.random.randint(jax.random.fold_in(stream_key, axis), (), 0, length) for axis, length in enumerate(values.shape)]
    main_axis = values.shape.index(max(values.shape))
    beside = spot[:main_axis] + [(spot[main_axis] + 1) % values.shape[main_axis]] + spot[main_axis + 1:]
    return values.at[tuple(spot)].set(smallest).at[tuple(beside)].set(top_value)


def shard_levels(rng, dims, cuts, least, top_value):
    gain, own = 1.0, jax.random.fold_in(rng, 6)
    for axis_at, shards_of in cuts:
        steps = jnp.exp(jax.random.uniform(jax.random.fold_in(own, axis_at), (shards_of,), jnp.float32, least / len(cuts), top_value / len(cuts)))
        gain = gain * jnp.repeat(steps, dims[axis_at] // shards_of).reshape([-1 if axis == axis_at else 1 for axis in range(len(dims))])
    return gain


def scatter_about(rng, dims, width, limit, cuts=(), held_as=jnp.bfloat16):
    level = shard_levels(rng, dims, cuts, -0.22, 0.18) if cuts else 1.0
    array = jax.random.normal(rng, dims, jnp.float32) * width * level
    return jnp.minimum(jnp.maximum(array, -limit), limit).astype(held_as)


def setup_inputs(seed: int = 0) -> dict:
    key_list = jax.random.split(jax.random.key(seed), 10)
    return {
        "q_latent": scatter_about(key_list[0], (ROWS, QLORA), 1.0, 6.0, ((0, 256),)),
        "draft_latent": scatter_about(key_list[1], (ROWS, KVL), 1.0, 6.0, ((0, 256),)),
        "draft_rope": scatter_about(key_list[2], (ROWS, ROPE), 1.0, 6.0, ((0, 256),)),
        "draft_start": set_ends(jax.random.randint(key_list[3], (SAMPLES_GRP * N_GRP,), 0, DRAFT), jax.random.fold_in(key_list[3], 1), 0, DRAFT - 1).astype(jnp.int32),
        "prompt_latent": draw_prompt_latent(jax.random.fold_in(key_list[9], 71), 0),
        "prompt_rope": scatter_about(key_list[5], (PROMPT, ROPE), 1.0, 6.0, ((0, 256),)),
        "w_uq": scatter_about(key_list[6], (QLORA, HEADS * (NOPE + ROPE)), QLORA ** -0.5, 0.15625, ((1, 16),)),
        "w_uk": scatter_about(key_list[7], (HEADS, NOPE, KVL), NOPE ** -0.5, 0.5, ((0, 16),)),
        "w_uv": scatter_about(key_list[8], (HEADS, KVL, VD), KVL ** -0.5, 0.25, ((0, 16),)),
    }


def rotate(rope_q, positions):
    half = ROPE // 2
    freq = 10000.0 ** (-jnp.arange(half, dtype=jnp.float32) / half)
    angle = positions[:, None].astype(jnp.float32) * freq[None, :]
    cosine = jnp.cos(angle)[:, None, :]
    sine = jnp.sin(angle)[:, None, :]
    values = rope_q.astype(jnp.float32)
    first = values[..., :half]
    second = values[..., half:]
    return jnp.concatenate([first * cosine - second * sine, second * cosine + first * sine], axis=-1).astype(jnp.bfloat16)


def draft_bias(starts, count):
    rows = jnp.arange(count, dtype=jnp.int32)
    same = (rows[:, None] // DRAFT) == (rows[None, :] // DRAFT)
    key_start = jnp.repeat(starts, DRAFT)
    upper = (rows[None, :] % DRAFT) <= (rows[:, None] % DRAFT)
    lower = key_start[None, :] <= (rows[None, :] % DRAFT)
    return jnp.where(same & upper & lower, 0.0, -1e30).astype(jnp.float32)


def attend_group(q_rows, d_lat, d_rope, starts, prompt_latent, prompt_rope, w_uq, w_uk, w_uv):
    count = q_rows.shape[0]
    heads = w_uk.shape[0]
    q_full = jnp.dot(q_rows, w_uq, preferred_element_type=jnp.float32).astype(jnp.bfloat16)
    q_full = q_full.reshape(count, heads, NOPE + ROPE)
    positions = PROMPT + jnp.arange(count, dtype=jnp.int32) % DRAFT
    q_rot = rotate(q_full[..., NOPE:], positions)
    q_abs = jnp.einsum("rhd,hdc->rhc", q_full[..., :NOPE].astype(jnp.float32), w_uk.astype(jnp.float32)).astype(jnp.bfloat16)
    q_abs = q_abs.reshape(count * heads, KVL)
    q_rot = q_rot.reshape(count * heads, ROPE)
    scale = 1.0 / (NOPE + ROPE) ** 0.5
    s_prompt = (jnp.dot(q_abs, prompt_latent.T, preferred_element_type=jnp.float32) + jnp.dot(q_rot, prompt_rope.T, preferred_element_type=jnp.float32)) * scale
    s_draft = (jnp.dot(q_abs, d_lat.T, preferred_element_type=jnp.float32) + jnp.dot(q_rot, d_rope.T, preferred_element_type=jnp.float32)) * scale
    s_draft = (s_draft.reshape(count, heads, count) + draft_bias(starts, count)[:, None, :]).reshape(count * heads, count)
    top = jnp.maximum(jnp.max(s_prompt, axis=1), jnp.max(s_draft, axis=1))
    e_prompt = jnp.exp(s_prompt - top[:, None])
    e_draft = jnp.exp(s_draft - top[:, None])
    total = jnp.sum(e_prompt, axis=1) + jnp.sum(e_draft, axis=1)
    summed = jnp.dot(e_prompt.astype(jnp.bfloat16), prompt_latent, preferred_element_type=jnp.float32) + jnp.dot(e_draft.astype(jnp.bfloat16), d_lat, preferred_element_type=jnp.float32)
    context = (summed / total[:, None]).astype(jnp.bfloat16).reshape(count, heads, KVL)
    output = jnp.einsum("rhc,hcv->rhv", context.astype(jnp.float32), w_uv.astype(jnp.float32)).astype(jnp.bfloat16)
    return output.reshape(count, heads * VD)


def reference(q_latent, draft_latent, draft_rope, draft_start, prompt_latent, prompt_rope, w_uq, w_uk, w_uv):
    count = SAMPLES_GRP * DRAFT
    q_groups = q_latent.reshape(N_GRP, count, QLORA)
    lat_groups = draft_latent.reshape(N_GRP, count, KVL)
    rope_groups = draft_rope.reshape(N_GRP, count, ROPE)
    start_groups = draft_start.reshape(N_GRP, SAMPLES_GRP)

    def one_group(items):
        return attend_group(items[0], items[1], items[2], items[3], prompt_latent, prompt_rope, w_uq, w_uk, w_uv)

    outputs = lax.map(one_group, (q_groups, lat_groups, rope_groups, start_groups))
    return outputs.reshape(N_GRP * count, w_uk.shape[0] * VD)
```

```python
import math

import jax
import jax.numpy as jnp
import numpy as np
from jax import lax
from jax.experimental import pallas as pl
from jax.experimental.pallas import tpu as pltpu
from jax.sharding import PartitionSpec as P

MESH = pl.DeviceIdType.MESH
KVL = 512
ROPE = 64
NOPE = 128
VD = 128
DRAFT = 8
PROMPT = 8192
QLORA = 1536
ROWS = 64
HEADS = 8
GROUP = ROWS * HEADS
SCALE = math.log2(math.e) / math.sqrt(NOPE + ROPE)
UNIT = 9
UNITS = 128
BLOCK = 256
NT = (((1,), (1,)), ((), ()))


def rotation_table():
    half = ROPE // 2
    freq = np.float32(10000.0) ** (-np.arange(half, dtype=np.float32) / np.float32(half))
    position = PROMPT + np.arange(DRAFT, dtype=np.float32)
    angle = (position[:, None] * freq[None, :].astype(np.float32)).astype(np.float64)
    zero = np.zeros((DRAFT, 2 * half))
    cosine = np.concatenate([np.cos(angle), np.cos(angle), zero], axis=1)
    sine = np.concatenate([-np.sin(angle), np.sin(angle), zero], axis=1)
    return np.concatenate([cosine, sine], axis=0).astype(np.float32)


def early(bs, cs, as_):
    return (bs * 2 + cs) * 4 + as_


def late(bs, cs, as_, zs=0):
    return 32 + ((bs * 2 + cs) * 4 + as_) * 3 + zs


def chunks():
    both = (0, 1)
    first = [early(b, c, a) for c in both for b in range(3) for a in range(4)]
    first += [early(3, c, 0) for c in both] + [late(0, c, 0, z) for c in both for z in range(3)]
    second = [late(b, c, a, z) for c in both for b, a in ((0, 1), (0, 2), (0, 3), (1, 0), (2, 0)) for z in range(3)]
    second += [early(3, c, 3) for c in both]
    third = [late(b, c, 1, z) for c in both for b in (1, 2) for z in range(3)]
    third += [late(b, c, 2, z) for c in both for b in (1, 2) for z in range(3)]
    fourth = [late(b, c, 3, z) for c in both for b in (1, 2) for z in range(3)]
    fourth += [late(3, c, 0, z) for c in both for z in range(3)]
    fourth += [early(3, c, a) for c in both for a in (1, 2)] + [late(3, c, 1, 0) for c in both]
    fifth = [late(3, c, 1, z) for c in both for z in (1, 2)]
    fifth += [late(3, c, a, z) for c in both for a in (2, 3) for z in range(3)]
    return first, second, third, fourth, fifth


def dot_t(a, b):
    return lax.dot_general(a, b, NT, preferred_element_type=jnp.float32)


def dot(a, b):
    return jnp.dot(a, b, preferred_element_type=jnp.float32)


def kernel(
    ql_ref, dl_ref, dr_ref, start_ref, pl_ref, pr_ref, table_ref, w_uq, w_uk, w_uv, out_ref,
    keys, q_send, q_all, q_stage, q_own, q_peer, q_full, queries, draft, acc, top, total,
    o_send, o_recv, s_send, s_recv, v_uq, v_uk, v_uv, local_sem, send_sem, recv_sem,
):
    grp, head = lax.axis_index("grp"), lax.axis_index("head")
    x, y, z, core = head // 4, (grp // 8) * 2 + (head // 2) % 2, grp % 8, head % 2
    toward = 2 * (z % 2) - 1

    def place(px, py, pz, pc):
        return ((py // 2) * 8 + pz, px * 4 + (py % 2) * 2 + pc)

    def at_a(step):
        return place((x + step * core + 4) % 4, (y + step * (1 - core) + 4) % 4, z, core)

    def at_b(step):
        return place((x + step * (1 - core) + 4) % 4, (y + step * core + 4) % 4, z, core)

    def at_z(step):
        return place(x, y, (z + step + 8) % 8, core)

    beside = y + 1 - 2 * (y % 2)
    sibling = place(x, y, z, 1 - core)
    partner = at_z(-toward)
    q_peers = [place((x + dx) % 4, y, z, core) for dx in (1, 3, 2)]
    q_peers += [place((x + dx) % 4, beside, z, core) for dx in (0, 1, 3, 2)]
    greeted = q_peers + [place(x, (y + 3 + 2 * (y % 2)) % 4, z, core), place(x, (y + 2) % 4, z, core)]
    greeted += [at_z(toward), at_z(3 * toward), at_z(2), at_z(-2), partner, sibling]

    weights = [
        pltpu.make_async_copy(src, dst, local_sem.at[i])
        for i, (src, dst) in enumerate(((w_uq, v_uq), (w_uk, v_uk), (w_uv, v_uv)))
    ]
    for copy in weights:
        copy.start()
    barrier = pltpu.get_barrier_semaphore()
    for device in greeted:
        pl.semaphore_signal(barrier, inc=1, device_id=device, device_id_type=MESH)

    sent = []

    def send(src, dst, device):
        i = len(sent)
        copy = pltpu.make_async_remote_copy(
            src_ref=src, dst_ref=dst, send_sem=send_sem.at[i], recv_sem=recv_sem.at[i],
            device_id=device, device_id_type=MESH,
        )
        copy.start()
        sent.append(copy)
        return copy

    def tiles(unit, count=1, first=0, last=0):
        return keys.at[pl.ds(unit * UNIT + first, count * UNIT - first - last)]

    def move(src, dst, count, device, first=0, last=0):
        return send(tiles(src, count, first, last), tiles(dst, count, first, last), device)

    for row in range(2):
        for lane in range(4):
            keys[early(0, 0, 0) * UNIT + row * 4 + lane] = pl_ref[row * 16 : row * 16 + 16, lane * 128 : lane * 128 + 128]
    keys[early(0, 0, 0) * UNIT + 8] = jnp.concatenate([pr_ref[0:16, :], pr_ref[16:32, :]], axis=1)
    q_stage[...] = jnp.zeros(q_stage.shape, jnp.float32)
    for part in range(4):
        q_stage[part * 4 : part * 4 + 4, 0:384] = ql_ref[:, part * 384 : part * 384 + 384].astype(jnp.float32)
        q_stage[part * 4 : part * 4 + 4, 384:512] = dl_ref[:, part * 128 : part * 128 + 128].astype(jnp.float32)
    q_stage[0:4, 512:576] = dr_ref[...].astype(jnp.float32)
    q_send[...] = q_stage[...].astype(jnp.bfloat16)
    my_rows = pl.ds(pl.multiple_of((core * 8 + head // 2) * 16, 16), 16)
    q_all[my_rows, :] = q_send[...]

    pl.semaphore_wait(barrier, len(greeted))

    q_copies = [send(q_send, q_all.at[my_rows, :], device) for device in q_peers]
    z_copies = [
        move(early(0, 0, 0), late(0, 0, 0, slot), 1, at_z(step))
        for slot, step in enumerate((toward, -2 * toward, 3 * toward))
    ]

    class Stream:
        def __init__(self, unit, count):
            self.unit, self.count = unit, count
            self.right, self.left, self.far = [None] * 4, [None] * 4, [None] * 8
            self.side = []

        def start(self):
            unit, count = self.unit, self.count
            own = unit(0, 0, 0)
            self.a = [move(own, unit(0, 0, slot), count, at_a(step)) for slot, step in ((1, 1), (2, -1), (3, 2))]
            self.spread(0)
            self.to_sibling(0, 0, 1)

        def spread(self, k):
            unit, count = self.unit, self.count
            self.right[k] = move(unit(0, 0, k), unit(1, 0, k), count, at_b(1))
            self.left[k] = move(unit(0, 0, k), unit(2, 0, k), count, at_b(-1))

        def to_sibling(self, bs, k, width):
            unit, count = self.unit, self.count
            self.side.append(move(unit(bs, 0, k), unit(bs, 1, k), count * width, sibling))

        def arrive_a(self):
            for k in (1, 2, 3):
                self.a[k - 1].wait_recv()
                self.spread(k)
            self.to_sibling(0, 1, 3)

        def arrive_b(self, ks):
            unit, count = self.unit, self.count
            cut = count * UNIT // 2
            for k in ks:
                self.right[k].wait_recv()
                self.far[2 * k] = move(unit(1, 0, k), unit(3, 0, k), count, at_b(1), 0, count * UNIT - cut)
                self.left[k].wait_recv()
                self.far[2 * k + 1] = move(unit(2, 0, k), unit(3, 0, k), count, at_b(-1), cut, 0)
            self.to_sibling(1, ks[0], len(ks))
            self.to_sibling(2, ks[0], len(ks))

        def arrive_far(self, ks):
            for k in ks:
                self.far[2 * k].wait_recv()
                self.far[2 * k + 1].wait_recv()
            self.to_sibling(3, ks[0], len(ks))

        def arrive_sibling(self, count):
            for _ in range(count):
                self.side.pop(0).wait_recv()

    soon, later = Stream(early, 1), Stream(late, 3)
    soon.start()

    soon.arrive_a()
    for copy in z_copies:
        copy.wait_recv()
    later.start()
    for copy in q_copies:
        copy.wait_recv()
    half = pl.ds(pl.multiple_of(core * 128, 128), 128)
    q_side = send(q_all.at[half, :], q_all.at[half, :], sibling)
    soon.arrive_b([0])
    q_side.wait_recv()

    row_at = lax.broadcasted_iota(jnp.int32, (ROWS, 256), 0)
    col_at = lax.broadcasted_iota(jnp.int32, (ROWS, 256), 1)
    from_head = row_at // 4
    source = ((from_head % 2) * 8 + from_head // 2) * 16 + row_at % 4
    for part in range(4):
        pick = jnp.where(col_at == source + part * 4, 1.0, 0.0).astype(jnp.bfloat16)
        picked = dot(pick, q_all[...]).astype(jnp.bfloat16)
        q_own[:, part * 384 : part * 384 + 384] = picked[:, 0:384]
        draft[:, 128 + part * 128 : 256 + part * 128] = picked[:, 384:512]
        if part == 0:
            draft[:, 0:128] = picked[:, 512:640]
    q_peer_copy = send(q_own, q_peer, partner)

    lane = lax.broadcasted_iota(jnp.int32, (ROWS, 128), 1)

    def project(group, rows_ref):
        q_full[...] = dot(rows_ref[...], v_uq[...]).astype(jnp.bfloat16).astype(jnp.float32)
        cosine = jnp.concatenate([table_ref[0:8, :]] * 8, axis=0)
        sine = jnp.concatenate([table_ref[8:16, :]] * 8, axis=0)

        def absorb(h, nope, pe):
            rows = pl.ds(group * GROUP + h * ROWS, ROWS)
            turned = jnp.where(lane < 32, pltpu.roll(pe, 96, 1), pltpu.roll(pe, 32, 1))
            rotated = pe * cosine + turned * sine
            queries[rows, 0:128] = rotated.astype(jnp.bfloat16)
            queries[rows, 640:768] = pltpu.roll(rotated, 64, 1).astype(jnp.bfloat16)
            queries[rows, 128:640] = dot(nope.astype(jnp.bfloat16), v_uk[h]).astype(jnp.bfloat16)

        for pair in range(HEADS // 2):
            at = pair * 384
            middle = q_full[:, at + 128 : at + 256]
            end = pltpu.roll(q_full[:, at + 256 : at + 384], 64, 1)
            absorb(2 * pair, q_full[:, at : at + 128], middle)
            absorb(2 * pair + 1, jnp.where(lane < 64, pltpu.roll(middle, 64, 1), end), end)

    def score(rows, units):
        first, second = [], []
        low = [jnp.concatenate([keys[u * UNIT + t] for u in units], axis=0) for t in range(4)]
        high = [jnp.concatenate([keys[u * UNIT + 4 + t] for u in units], axis=0) for t in range(4)]
        rope = jnp.concatenate([keys[u * UNIT + 8] for u in units], axis=0)
        left = dot_t(queries[rows, 0:640], jnp.concatenate([rope] + low, axis=1))
        right = dot_t(queries[rows, 128:768], jnp.concatenate(high + [rope], axis=1))
        values = jnp.concatenate([jnp.concatenate(low, axis=1), jnp.concatenate(high, axis=1)], axis=0)
        return jnp.concatenate([left, right], axis=1) * SCALE, values

    def update(rows, scores, values, first=False):
        peak = jnp.max(scores, axis=1, keepdims=True)
        if first:
            new_top = jnp.broadcast_to(peak, (BLOCK, 128))
        else:
            old_top = top[rows, :]
            new_top = jnp.maximum(old_top, peak)
            factor = jnp.exp2(old_top - new_top)
        e = jnp.exp2(scores - new_top[:, 0:1])
        part = jnp.sum(e, axis=1, keepdims=True)
        summed = dot(e.astype(jnp.bfloat16), values)
        if first:
            total[rows, :] = jnp.broadcast_to(part, (BLOCK, 128))
            acc[rows, :] = summed
        else:
            total[rows, :] = total[rows, :] * factor + part
            acc[rows, :] = acc[rows, :] * factor[:, 0:1] + summed
        top[rows, :] = new_top

    def attend(items):
        held = None
        for group, block, units, first in items:
            rows = pl.ds(group * GROUP + block * BLOCK, BLOCK)
            now = (rows, *score(rows, units), first)
            if held is not None:
                update(*held)
            held = now
        update(*held)

    def attend_draft():
        row = lax.broadcasted_iota(jnp.int32, (BLOCK, ROWS), 0) % ROWS
        col = lax.broadcasted_iota(jnp.int32, (BLOCK, ROWS), 1)
        begin = jnp.zeros((BLOCK, ROWS), jnp.int32)
        for i in range(8):
            begin = jnp.where(col // DRAFT == i, start_ref[i], begin)
        seen = (row // DRAFT == col // DRAFT) & (col % DRAFT <= row % DRAFT) & (begin <= col % DRAFT)
        bias = jnp.where(seen, 0.0, -1e30)
        for block in range(2):
            rows = pl.ds(block * BLOCK, BLOCK)
            scores = dot_t(queries[rows, 0:640], draft[...]) * SCALE + bias
            update(rows, scores, draft[:, 128:640], True)

    def context(group, h):
        rows = pl.ds(group * GROUP + h * ROWS, ROWS)
        ctx = (acc[rows, :] * (1.0 / total[rows, 0:1])).astype(jnp.bfloat16)
        return dot(ctx, v_uv[h]), top[rows, :] + jnp.log2(total[rows, :])

    c0, c1, c2, c3, c4 = chunks()
    weights[0].wait()
    weights[1].wait()
    project(0, q_own)
    soon.arrive_b([1, 2, 3])
    attend_draft()
    soon.arrive_far([0])
    later.arrive_a()
    later.arrive_b([0])
    soon.arrive_far([1, 2, 3])
    soon.arrive_sibling(8)
    later.arrive_sibling(1)
    attend([(0, 0, c0, False), (0, 1, c0, False)])
    later.arrive_b([1])
    q_peer_copy.wait_recv()
    project(1, q_peer)
    later.arrive_b([2])
    later.arrive_sibling(3)
    attend([(0, 0, c1, False), (0, 1, c1, False)])
    later.arrive_b([3])
    later.arrive_far([0])
    attend([(1, 0, c0, True), (1, 1, c0, True), (1, 0, c1, False), (1, 1, c1, False)])
    later.arrive_far([1])
    later.arrive_sibling(4)
    attend([(1, 0, c2, False), (1, 1, c2, False)])
    later.arrive_far([2, 3])
    later.arrive_sibling(4)
    attend([(1, 0, c3, False), (1, 1, c3, False)])
    later.arrive_sibling(1)
    attend([(1, 0, c4, False), (1, 1, c4, False)])
    weights[2].wait()
    shares = jnp.zeros((ROWS, 128), jnp.float32)
    for h in range(HEADS):
        value, share = context(1, h)
        o_send[:, h * VD : h * VD + VD] = value.astype(jnp.bfloat16)
        shares = jnp.where(lane == h, share, shares)
    s_send[...] = shares
    o_copy = send(o_send, o_recv, partner)
    s_copy = send(s_send, s_recv, partner)
    attend([(0, b, c, False) for c in (c2, c3, c4) for b in range(2)])
    own = [context(0, h) for h in range(HEADS)]
    o_copy.wait_recv()
    s_copy.wait_recv()
    for h, (value, share) in enumerate(own):
        other = jnp.broadcast_to(s_recv[:, h : h + 1], (ROWS, 128))
        mine = 1.0 / (1.0 + jnp.exp2(jnp.minimum(other - share, 120.0)))
        theirs = 1.0 / (1.0 + jnp.exp2(jnp.minimum(share - other, 120.0)))
        peer = o_recv[:, h * VD : h * VD + VD].astype(jnp.float32)
        out_ref[:, h * VD : h * VD + VD] = (value * mine + peer * theirs).astype(jnp.bfloat16)
    for copy in sent:
        copy.wait_send()


def on_device(
    q_latent, draft_latent, draft_rope, draft_start, prompt_latent, prompt_rope, w_uq, w_uk, w_uv
):
    vmem = pl.BlockSpec(memory_space=pltpu.VMEM)
    smem = pl.BlockSpec(memory_space=pltpu.SMEM)
    hbm = pl.BlockSpec(memory_space=pl.ANY)
    bf16, f32 = jnp.bfloat16, jnp.float32
    return pl.pallas_call(
        kernel,
        name="attention",
        out_shape=jax.ShapeDtypeStruct((ROWS, HEADS * VD), bf16),
        in_specs=[vmem, vmem, vmem, smem, vmem, vmem, vmem, hbm, hbm, hbm],
        out_specs=vmem,
        scratch_shapes=[
            pltpu.VMEM((UNITS * UNIT, 16, 128), bf16),
            pltpu.VMEM((16, 640), bf16),
            pltpu.VMEM((256, 640), bf16),
            pltpu.VMEM((16, 640), f32),
            pltpu.VMEM((ROWS, QLORA), bf16),
            pltpu.VMEM((ROWS, QLORA), bf16),
            pltpu.VMEM((ROWS, QLORA), f32),
            pltpu.VMEM((2 * GROUP, 768), bf16),
            pltpu.VMEM((ROWS, 640), bf16),
            pltpu.VMEM((2 * GROUP, KVL), f32),
            pltpu.VMEM((2 * GROUP, 128), f32),
            pltpu.VMEM((2 * GROUP, 128), f32),
            pltpu.VMEM((ROWS, HEADS * VD), bf16),
            pltpu.VMEM((ROWS, HEADS * VD), bf16),
            pltpu.VMEM((ROWS, 128), f32),
            pltpu.VMEM((ROWS, 128), f32),
            pltpu.VMEM((QLORA, HEADS * (NOPE + ROPE)), bf16),
            pltpu.VMEM((HEADS, NOPE, KVL), bf16),
            pltpu.VMEM((HEADS, KVL, VD), bf16),
            pltpu.SemaphoreType.DMA((3,)),
            pltpu.SemaphoreType.DMA((80,)),
            pltpu.SemaphoreType.DMA((80,)),
        ],
        compiler_params=pltpu.CompilerParams(
            collective_id=0, has_side_effects=True, vmem_limit_bytes=48 * 2**20
        ),
    )(
        q_latent, draft_latent, draft_rope, draft_start, prompt_latent, prompt_rope,
        rotation_table(), w_uq, w_uk, w_uv,
    )


def solution(mesh):
    in_specs = (
        P(("grp", "head"), None),
        P(("grp", "head"), None),
        P(("grp", "head"), None),
        P("grp"),
        P(("grp", "head"), None),
        P(("grp", "head"), None),
        P(None, "head"),
        P("head", None, None),
        P("head", None, None),
    )
    out_specs = P("grp", "head")
    return jax.shard_map(
        on_device, mesh=mesh, in_specs=in_specs, out_specs=out_specs, check_vma=False
    )
```

```python
import math

import jax
import jax.numpy as jnp
import numpy as np
from jax import lax
from jax.experimental import pallas as pl
from jax.experimental.pallas import tpu as pltpu
from jax.sharding import PartitionSpec as P

MESH = pl.DeviceIdType.MESH
KVL = 512
ROPE = 64
NOPE = 128
VD = 128
DRAFT = 8
PROMPT = 8192
QLORA = 1536
ROWS = 64
HEADS = 8
GROUP = ROWS * HEADS
SCALE = math.log2(math.e) / math.sqrt(NOPE + ROPE)
UNIT = 9
UNITS = 128
BLOCK = 256
NT = (((1,), (1,)), ((), ()))


def rotation_table():
    half = ROPE // 2
    freq = np.float32(10000.0) ** (-np.arange(half, dtype=np.float32) / np.float32(half))
    position = PROMPT + np.arange(DRAFT, dtype=np.float32)
    angle = (position[:, None] * freq[None, :].astype(np.float32)).astype(np.float64)
    zero = np.zeros((DRAFT, 2 * half))
    cosine = np.concatenate([np.cos(angle), np.cos(angle), zero], axis=1)
    sine = np.concatenate([-np.sin(angle), np.sin(angle), zero], axis=1)
    return np.concatenate([cosine, sine], axis=0).astype(np.float32)


def early(bs, cs, as_):
    return (bs * 2 + cs) * 4 + as_


def late(bs, cs, as_, zs=0):
    return 32 + ((bs * 2 + cs) * 4 + as_) * 3 + zs


def chunks():
    both = (0, 1)
    first = [early(b, c, a) for c in both for b in range(3) for a in range(4)]
    first += [early(3, c, 0) for c in both] + [late(0, c, 0, z) for c in both for z in range(3)]
    second = [late(b, c, a, z) for c in both for b, a in ((0, 1), (0, 2), (0, 3), (1, 0), (2, 0)) for z in range(3)]
    second += [early(3, c, 3) for c in both]
    third = [late(b, c, 1, z) for c in both for b in (1, 2) for z in range(3)]
    third += [late(b, c, 2, z) for c in both for b in (1, 2) for z in range(3)]
    fourth = [late(b, c, 3, z) for c in both for b in (1, 2) for z in range(3)]
    fourth += [late(3, c, 0, z) for c in both for z in range(3)]
    fourth += [early(3, c, a) for c in both for a in (1, 2)] + [late(3, c, 1, 0) for c in both]
    fifth = [late(3, c, 1, z) for c in both for z in (1, 2)]
    fifth += [late(3, c, a, z) for c in both for a in (2, 3) for z in range(3)]
    return first, second, third, fourth, fifth


def dot_t(a, b):
    return lax.dot_general(a, b, NT, preferred_element_type=jnp.float32)


def dot(a, b):
    return jnp.dot(a, b, preferred_element_type=jnp.float32)


def kernel(
    ql_in, dl_in, dr_in, start_in, pl_in, pr_in, table_in, w_uq, w_uk, w_uv, out_ref,
    ql_ref, dl_ref, dr_ref, start_ref, pl_ref, pr_ref, table_ref,
    keys, q_send, q_all, q_stage, q_own, q_peer, q_full, queries, draft, acc, top, total,
    o_send, o_recv, s_send, s_recv, v_uq, v_uk, v_uv, local_sem, send_sem, recv_sem,
):
    grp, head = lax.axis_index("grp"), lax.axis_index("head")
    x, y, z, core = head // 4, (grp // 8) * 2 + (head // 2) % 2, grp % 8, head % 2
    toward = 2 * (z % 2) - 1

    def place(px, py, pz, pc):
        return ((py // 2) * 8 + pz, px * 4 + (py % 2) * 2 + pc)

    def at_a(step):
        return place((x + step * core + 4) % 4, (y + step * (1 - core) + 4) % 4, z, core)

    def at_b(step):
        return place((x + step * (1 - core) + 4) % 4, (y + step * core + 4) % 4, z, core)

    def at_z(step):
        return place(x, y, (z + step + 8) % 8, core)

    beside = y + 1 - 2 * (y % 2)
    sibling = place(x, y, z, 1 - core)
    partner = at_z(-toward)
    q_peers = [place((x + dx) % 4, y, z, core) for dx in (1, 3, 2)]
    q_peers += [place((x + dx) % 4, beside, z, core) for dx in (0, 1, 3, 2)]
    greeted = q_peers + [place(x, (y + 3 + 2 * (y % 2)) % 4, z, core), place(x, (y + 2) % 4, z, core)]
    greeted += [at_z(toward), at_z(3 * toward), at_z(2), at_z(-2), partner, sibling]

    loads = [
        pltpu.make_async_copy(src, dst, local_sem.at[i])
        for i, (src, dst) in enumerate((
            (pl_in, pl_ref), (pr_in, pr_ref), (ql_in, ql_ref), (dl_in, dl_ref), (dr_in, dr_ref),
            (table_in, table_ref), (start_in, start_ref), (w_uq, v_uq), (w_uk, v_uk), (w_uv, v_uv),
        ))
    ]
    inputs, weights = loads[:7], loads[7:]
    for copy in inputs:
        copy.start()
    barrier = pltpu.get_barrier_semaphore()
    for device in greeted:
        pl.semaphore_signal(barrier, inc=1, device_id=device, device_id_type=MESH)
    for copy in weights:
        copy.start()
    for copy in inputs:
        copy.wait()

    sent = []

    def send(src, dst, device):
        i = len(sent)
        copy = pltpu.make_async_remote_copy(
            src_ref=src, dst_ref=dst, send_sem=send_sem.at[i], recv_sem=recv_sem.at[i],
            device_id=device, device_id_type=MESH,
        )
        copy.start()
        sent.append(copy)
        return copy

    def tiles(unit, count=1, first=0, last=0):
        return keys.at[pl.ds(unit * UNIT + first, count * UNIT - first - last)]

    def move(src, dst, count, device, first=0, last=0):
        return send(tiles(src, count, first, last), tiles(dst, count, first, last), device)

    for row in range(2):
        for lane in range(4):
            keys[early(0, 0, 0) * UNIT + row * 4 + lane] = pl_ref[row * 16 : row * 16 + 16, lane * 128 : lane * 128 + 128]
    keys[early(0, 0, 0) * UNIT + 8] = jnp.concatenate([pr_ref[0:16, :], pr_ref[16:32, :]], axis=1)
    q_stage[...] = jnp.zeros(q_stage.shape, jnp.float32)
    for part in range(4):
        q_stage[part * 4 : part * 4 + 4, 0:384] = ql_ref[:, part * 384 : part * 384 + 384].astype(jnp.float32)
        q_stage[part * 4 : part * 4 + 4, 384:512] = dl_ref[:, part * 128 : part * 128 + 128].astype(jnp.float32)
    q_stage[0:4, 512:576] = dr_ref[...].astype(jnp.float32)
    q_send[...] = q_stage[...].astype(jnp.bfloat16)
    my_rows = pl.ds(pl.multiple_of((core * 8 + head // 2) * 16, 16), 16)
    q_all[my_rows, :] = q_send[...]

    pl.semaphore_wait(barrier, len(greeted))

    q_copies = [send(q_send, q_all.at[my_rows, :], device) for device in q_peers]
    z_copies = [
        move(early(0, 0, 0), late(0, 0, 0, slot), 1, at_z(step))
        for slot, step in enumerate((toward, -2 * toward, 3 * toward))
    ]

    class Stream:
        def __init__(self, unit, count):
            self.unit, self.count = unit, count
            self.right, self.left, self.far = [None] * 4, [None] * 4, [None] * 8
            self.side = []

        def start(self):
            unit, count = self.unit, self.count
            own = unit(0, 0, 0)
            self.a = [move(own, unit(0, 0, slot), count, at_a(step)) for slot, step in ((1, 1), (2, -1), (3, 2))]
            self.spread(0)
            self.to_sibling(0, 0, 1)

        def spread(self, k):
            unit, count = self.unit, self.count
            self.right[k] = move(unit(0, 0, k), unit(1, 0, k), count, at_b(1))
            self.left[k] = move(unit(0, 0, k), unit(2, 0, k), count, at_b(-1))

        def to_sibling(self, bs, k, width):
            unit, count = self.unit, self.count
            self.side.append(move(unit(bs, 0, k), unit(bs, 1, k), count * width, sibling))

        def arrive_a(self):
            for k in (1, 2, 3):
                self.a[k - 1].wait_recv()
                self.spread(k)
            self.to_sibling(0, 1, 3)

        def arrive_b(self, ks):
            unit, count = self.unit, self.count
            cut = count * UNIT // 2
            for k in ks:
                self.right[k].wait_recv()
                self.far[2 * k] = move(unit(1, 0, k), unit(3, 0, k), count, at_b(1), 0, count * UNIT - cut)
                self.left[k].wait_recv()
                self.far[2 * k + 1] = move(unit(2, 0, k), unit(3, 0, k), count, at_b(-1), cut, 0)
            self.to_sibling(1, ks[0], len(ks))
            self.to_sibling(2, ks[0], len(ks))

        def arrive_far(self, ks):
            for k in ks:
                self.far[2 * k].wait_recv()
                self.far[2 * k + 1].wait_recv()
            self.to_sibling(3, ks[0], len(ks))

        def arrive_sibling(self, count):
            for _ in range(count):
                self.side.pop(0).wait_recv()

    soon, later = Stream(early, 1), Stream(late, 3)
    soon.start()

    soon.arrive_a()
    for copy in z_copies:
        copy.wait_recv()
    later.start()
    for copy in q_copies:
        copy.wait_recv()
    half = pl.ds(pl.multiple_of(core * 128, 128), 128)
    q_side = send(q_all.at[half, :], q_all.at[half, :], sibling)
    soon.arrive_b([0])
    q_side.wait_recv()

    row_at = lax.broadcasted_iota(jnp.int32, (ROWS, 256), 0)
    col_at = lax.broadcasted_iota(jnp.int32, (ROWS, 256), 1)
    from_head = row_at // 4
    source = ((from_head % 2) * 8 + from_head // 2) * 16 + row_at % 4
    for part in range(4):
        pick = jnp.where(col_at == source + part * 4, 1.0, 0.0).astype(jnp.bfloat16)
        picked = dot(pick, q_all[...]).astype(jnp.bfloat16)
        q_own[:, part * 384 : part * 384 + 384] = picked[:, 0:384]
        draft[:, 128 + part * 128 : 256 + part * 128] = picked[:, 384:512]
        if part == 0:
            draft[:, 0:128] = picked[:, 512:640]
    q_peer_copy = send(q_own, q_peer, partner)

    lane = lax.broadcasted_iota(jnp.int32, (ROWS, 128), 1)

    def project(group, rows_ref):
        q_full[...] = dot(rows_ref[...], v_uq[...]).astype(jnp.bfloat16).astype(jnp.float32)
        cosine = jnp.concatenate([table_ref[0:8, :]] * 8, axis=0)
        sine = jnp.concatenate([table_ref[8:16, :]] * 8, axis=0)

        def absorb(h, nope, pe):
            rows = pl.ds(group * GROUP + h * ROWS, ROWS)
            turned = jnp.where(lane < 32, pltpu.roll(pe, 96, 1), pltpu.roll(pe, 32, 1))
            rotated = pe * cosine + turned * sine
            queries[rows, 0:128] = rotated.astype(jnp.bfloat16)
            queries[rows, 640:768] = pltpu.roll(rotated, 64, 1).astype(jnp.bfloat16)
            queries[rows, 128:640] = dot(nope.astype(jnp.bfloat16), v_uk[h]).astype(jnp.bfloat16)

        for pair in range(HEADS // 2):
            at = pair * 384
            middle = q_full[:, at + 128 : at + 256]
            end = pltpu.roll(q_full[:, at + 256 : at + 384], 64, 1)
            absorb(2 * pair, q_full[:, at : at + 128], middle)
            absorb(2 * pair + 1, jnp.where(lane < 64, pltpu.roll(middle, 64, 1), end), end)

    def score(rows, units):
        first, second = [], []
        low = [jnp.concatenate([keys[u * UNIT + t] for u in units], axis=0) for t in range(4)]
        high = [jnp.concatenate([keys[u * UNIT + 4 + t] for u in units], axis=0) for t in range(4)]
        rope = jnp.concatenate([keys[u * UNIT + 8] for u in units], axis=0)
        left = dot_t(queries[rows, 0:640], jnp.concatenate([rope] + low, axis=1))
        right = dot_t(queries[rows, 128:768], jnp.concatenate(high + [rope], axis=1))
        values = jnp.concatenate([jnp.concatenate(low, axis=1), jnp.concatenate(high, axis=1)], axis=0)
        return jnp.concatenate([left, right], axis=1) * SCALE, values

    def update(rows, scores, values, first=False):
        peak = jnp.max(scores, axis=1, keepdims=True)
        if first:
            new_top = jnp.broadcast_to(peak, (BLOCK, 128))
        else:
            old_top = top[rows, :]
            new_top = jnp.maximum(old_top, peak)
            factor = jnp.exp2(old_top - new_top)
        e = jnp.exp2(scores - new_top[:, 0:1])
        part = jnp.sum(e, axis=1, keepdims=True)
        summed = dot(e.astype(jnp.bfloat16), values)
        if first:
            total[rows, :] = jnp.broadcast_to(part, (BLOCK, 128))
            acc[rows, :] = summed
        else:
            total[rows, :] = total[rows, :] * factor + part
            acc[rows, :] = acc[rows, :] * factor[:, 0:1] + summed
        top[rows, :] = new_top

    def attend(items):
        held = None
        for group, block, units, first in items:
            rows = pl.ds(group * GROUP + block * BLOCK, BLOCK)
            now = (rows, *score(rows, units), first)
            if held is not None:
                update(*held)
            held = now
        update(*held)

    def attend_draft():
        row = lax.broadcasted_iota(jnp.int32, (BLOCK, ROWS), 0) % ROWS
        col = lax.broadcasted_iota(jnp.int32, (BLOCK, ROWS), 1)
        begin = jnp.zeros((BLOCK, ROWS), jnp.int32)
        for i in range(8):
            begin = jnp.where(col // DRAFT == i, start_ref[i], begin)
        seen = (row // DRAFT == col // DRAFT) & (col % DRAFT <= row % DRAFT) & (begin <= col % DRAFT)
        bias = jnp.where(seen, 0.0, -1e30)
        for block in range(2):
            rows = pl.ds(block * BLOCK, BLOCK)
            scores = dot_t(queries[rows, 0:640], draft[...]) * SCALE + bias
            update(rows, scores, draft[:, 128:640], True)

    def context(group, h):
        rows = pl.ds(group * GROUP + h * ROWS, ROWS)
        ctx = (acc[rows, :] * (1.0 / total[rows, 0:1])).astype(jnp.bfloat16)
        return dot(ctx, v_uv[h]), top[rows, :] + jnp.log2(total[rows, :])

    c0, c1, c2, c3, c4 = chunks()
    weights[0].wait()
    weights[1].wait()
    project(0, q_own)
    soon.arrive_b([1, 2, 3])
    attend_draft()
    soon.arrive_far([0])
    later.arrive_a()
    later.arrive_b([0])
    soon.arrive_far([1, 2, 3])
    soon.arrive_sibling(8)
    later.arrive_sibling(1)
    attend([(0, 0, c0, False), (0, 1, c0, False)])
    later.arrive_b([1])
    q_peer_copy.wait_recv()
    project(1, q_peer)
    later.arrive_b([2])
    later.arrive_sibling(3)
    attend([(0, 0, c1, False), (0, 1, c1, False)])
    later.arrive_b([3])
    later.arrive_far([0])
    attend([(1, 0, c0, True), (1, 1, c0, True), (1, 0, c1, False), (1, 1, c1, False)])
    later.arrive_far([1])
    later.arrive_sibling(4)
    attend([(1, 0, c2, False), (1, 1, c2, False)])
    later.arrive_far([2, 3])
    later.arrive_sibling(4)
    attend([(1, 0, c3, False), (1, 1, c3, False)])
    later.arrive_sibling(1)
    attend([(1, 0, c4, False), (1, 1, c4, False)])
    weights[2].wait()
    shares = jnp.zeros((ROWS, 128), jnp.float32)
    for h in range(HEADS):
        value, share = context(1, h)
        o_send[:, h * VD : h * VD + VD] = value.astype(jnp.bfloat16)
        shares = jnp.where(lane == h, share, shares)
    s_send[...] = shares
    o_copy = send(o_send, o_recv, partner)
    s_copy = send(s_send, s_recv, partner)
    attend([(0, b, c, False) for c in (c2, c3, c4) for b in range(2)])
    own = [context(0, h) for h in range(HEADS)]
    o_copy.wait_recv()
    s_copy.wait_recv()
    for h, (value, share) in enumerate(own):
        other = jnp.broadcast_to(s_recv[:, h : h + 1], (ROWS, 128))
        mine = 1.0 / (1.0 + jnp.exp2(jnp.minimum(other - share, 120.0)))
        theirs = 1.0 / (1.0 + jnp.exp2(jnp.minimum(share - other, 120.0)))
        peer = o_recv[:, h * VD : h * VD + VD].astype(jnp.float32)
        out_ref[:, h * VD : h * VD + VD] = (value * mine + peer * theirs).astype(jnp.bfloat16)
    for copy in sent:
        copy.wait_send()


def on_device(
    q_latent, draft_latent, draft_rope, draft_start, prompt_latent, prompt_rope, w_uq, w_uk, w_uv
):
    vmem = pl.BlockSpec(memory_space=pltpu.VMEM)
    hbm = pl.BlockSpec(memory_space=pltpu.HBM)
    bf16, f32 = jnp.bfloat16, jnp.float32
    return pl.pallas_call(
        kernel,
        name="attention",
        out_shape=jax.ShapeDtypeStruct((ROWS, HEADS * VD), bf16),
        in_specs=[hbm] * 10,
        out_specs=vmem,
        scratch_shapes=[
            pltpu.VMEM((4, QLORA), bf16),
            pltpu.VMEM((4, KVL), bf16),
            pltpu.VMEM((4, ROPE), bf16),
            pltpu.SMEM((8,), jnp.int32),
            pltpu.VMEM((32, KVL), bf16),
            pltpu.VMEM((32, ROPE), bf16),
            pltpu.VMEM((16, 128), f32),
            pltpu.VMEM((UNITS * UNIT, 16, 128), bf16),
            pltpu.VMEM((16, 640), bf16),
            pltpu.VMEM((256, 640), bf16),
            pltpu.VMEM((16, 640), f32),
            pltpu.VMEM((ROWS, QLORA), bf16),
            pltpu.VMEM((ROWS, QLORA), bf16),
            pltpu.VMEM((ROWS, QLORA), f32),
            pltpu.VMEM((2 * GROUP, 768), bf16),
            pltpu.VMEM((ROWS, 640), bf16),
            pltpu.VMEM((2 * GROUP, KVL), f32),
            pltpu.VMEM((2 * GROUP, 128), f32),
            pltpu.VMEM((2 * GROUP, 128), f32),
            pltpu.VMEM((ROWS, HEADS * VD), bf16),
            pltpu.VMEM((ROWS, HEADS * VD), bf16),
            pltpu.VMEM((ROWS, 128), f32),
            pltpu.VMEM((ROWS, 128), f32),
            pltpu.VMEM((QLORA, HEADS * (NOPE + ROPE)), bf16),
            pltpu.VMEM((HEADS, NOPE, KVL), bf16),
            pltpu.VMEM((HEADS, KVL, VD), bf16),
            pltpu.SemaphoreType.DMA((10,)),
            pltpu.SemaphoreType.DMA((80,)),
            pltpu.SemaphoreType.DMA((80,)),
        ],
        compiler_params=pltpu.CompilerParams(
            collective_id=0, has_side_effects=True, vmem_limit_bytes=64 * 2**20
        ),
    )(
        q_latent, draft_latent, draft_rope, draft_start, prompt_latent, prompt_rope,
        rotation_table(), w_uq, w_uk, w_uv,
    )


def solution(mesh):
    in_specs = (
        P(("grp", "head"), None),
        P(("grp", "head"), None),
        P(("grp", "head"), None),
        P("grp"),
        P(("grp", "head"), None),
        P(("grp", "head"), None),
        P(None, "head"),
        P("head", None, None),
        P("head", None, None),
    )
    out_specs = P("grp", "head")
    return jax.shard_map(
        on_device, mesh=mesh, in_specs=in_specs, out_specs=out_specs, check_vma=False
    )
```

```python
import math

import jax
import jax.numpy as jnp
import numpy as np
from jax import lax
from jax.experimental import pallas as pl
from jax.experimental.pallas import tpu as pltpu
from jax.sharding import PartitionSpec as P

MESH = pl.DeviceIdType.MESH
KVL = 512
ROPE = 64
NOPE = 128
VD = 128
DRAFT = 8
PROMPT = 8192
QLORA = 1536
ROWS = 64
HEADS = 8
GROUP = ROWS * HEADS
SCALE = math.log2(math.e) / math.sqrt(NOPE + ROPE)
UNIT = 9
UNITS = 128
BLOCK = 256
NT = (((1,), (1,)), ((), ()))


def rotation_table():
    half = ROPE // 2
    freq = np.float32(10000.0) ** (-np.arange(half, dtype=np.float32) / np.float32(half))
    position = PROMPT + np.arange(DRAFT, dtype=np.float32)
    angle = (position[:, None] * freq[None, :].astype(np.float32)).astype(np.float64)
    zero = np.zeros((DRAFT, 2 * half))
    cosine = np.concatenate([np.cos(angle), np.cos(angle), zero], axis=1)
    sine = np.concatenate([-np.sin(angle), np.sin(angle), zero], axis=1)
    return np.concatenate([cosine, sine], axis=0).astype(np.float32)


def unit(stream, bs, cs, as_):
    return ((stream * 4 + bs) * 2 + cs) * 4 + as_


def chunk(streams, bss):
    return [unit(s, b, c, a) for s in streams for b in bss for c in (0, 1) for a in range(4)]


def dot_t(a, b):
    return lax.dot_general(a, b, NT, preferred_element_type=jnp.float32)


def dot(a, b):
    return jnp.dot(a, b, preferred_element_type=jnp.float32)


def kernel(
    ql_in, dl_in, dr_in, start_in, pl_in, pr_in, table_in, w_uq, w_uk, w_uv, out_ref,
    ql_ref, dl_ref, dr_ref, start_ref, pl_ref, pr_ref, table_ref,
    keys, q_send, q_all, q_stage, q_own, q_peer, q_full, queries, draft, acc, top, total,
    o_send, o_recv, s_send, s_recv, v_uq, v_uk, v_uv, local_sem, send_sem, recv_sem,
):
    grp, head = lax.axis_index("grp"), lax.axis_index("head")
    x, y, z, core = head // 4, (grp // 8) * 2 + (head // 2) % 2, grp % 8, head % 2
    toward = 2 * (z % 2) - 1

    def place(px, py, pz, pc):
        return ((py // 2) * 8 + pz, px * 4 + (py % 2) * 2 + pc)

    def at_a(step):
        return place((x + step * core + 4) % 4, (y + step * (1 - core) + 4) % 4, z, core)

    def at_b(step):
        return place((x + step * (1 - core) + 4) % 4, (y + step * core + 4) % 4, z, core)

    def at_z(step):
        return place(x, y, (z + step + 8) % 8, core)

    beside = y + 1 - 2 * (y % 2)
    sibling = place(x, y, z, 1 - core)
    partner = at_z(-toward)
    q_peers = [place((x + dx) % 4, y, z, core) for dx in (1, 3, 2)]
    q_peers += [place((x + dx) % 4, beside, z, core) for dx in (0, 1, 3, 2)]
    greeted = q_peers + [place(x, (y + 3 + 2 * (y % 2)) % 4, z, core), place(x, (y + 2) % 4, z, core)]
    greeted += [at_z(toward), at_z(3 * toward), at_z(2), at_z(-2), partner, sibling]

    loads = [
        pltpu.make_async_copy(src, dst, local_sem.at[i])
        for i, (src, dst) in enumerate((
            (pl_in, pl_ref), (pr_in, pr_ref), (ql_in, ql_ref), (dl_in, dl_ref), (dr_in, dr_ref),
            (table_in, table_ref), (start_in, start_ref), (w_uq, v_uq), (w_uk, v_uk), (w_uv, v_uv),
        ))
    ]
    inputs, weights = loads[:7], loads[7:]
    for copy in inputs:
        copy.start()
    barrier = pltpu.get_barrier_semaphore()
    for device in greeted:
        pl.semaphore_signal(barrier, inc=1, device_id=device, device_id_type=MESH)
    for copy in weights:
        copy.start()
    for copy in inputs:
        copy.wait()

    sent = []

    def send(src, dst, device):
        i = len(sent)
        copy = pltpu.make_async_remote_copy(
            src_ref=src, dst_ref=dst, send_sem=send_sem.at[i], recv_sem=recv_sem.at[i],
            device_id=device, device_id_type=MESH,
        )
        copy.start()
        sent.append(copy)
        return copy

    def tiles(at, count=1, first=0, last=0):
        return keys.at[pl.ds(at * UNIT + first, count * UNIT - first - last)]

    def move(src, dst, count, device, first=0, last=0):
        return send(tiles(src, count, first, last), tiles(dst, count, first, last), device)

    for row in range(2):
        for lane in range(4):
            keys[row * 4 + lane] = pl_ref[row * 16 : row * 16 + 16, lane * 128 : lane * 128 + 128]
    keys[8] = jnp.concatenate([pr_ref[0:16, :], pr_ref[16:32, :]], axis=1)
    q_stage[...] = jnp.zeros(q_stage.shape, jnp.float32)
    for part in range(4):
        q_stage[part * 4 : part * 4 + 4, 0:384] = ql_ref[:, part * 384 : part * 384 + 384].astype(jnp.float32)
        q_stage[part * 4 : part * 4 + 4, 384:512] = dl_ref[:, part * 128 : part * 128 + 128].astype(jnp.float32)
    q_stage[0:4, 512:576] = dr_ref[...].astype(jnp.float32)
    q_send[...] = q_stage[...].astype(jnp.bfloat16)
    my_rows = pl.ds(pl.multiple_of((core * 8 + head // 2) * 16, 16), 16)
    q_all[my_rows, :] = q_send[...]

    pl.semaphore_wait(barrier, len(greeted))

    q_copies = [send(q_send, q_all.at[my_rows, :], device) for device in q_peers]
    z_copies = [
        move(unit(0, 0, 0, 0), unit(stream, 0, 0, 0), 1, at_z(step))
        for stream, step in ((1, toward), (2, -2 * toward), (3, 3 * toward))
    ]

    class Stream:
        def __init__(self, index):
            self.index = index
            self.a, self.right, self.left = [None] * 4, [None] * 4, [None] * 4
            self.far = []
            self.side = [None] * 4

        def spread(self, k):
            own = unit(self.index, 0, 0, k)
            self.right[k] = move(own, unit(self.index, 1, 0, k), 1, at_b(1))
            self.left[k] = move(own, unit(self.index, 2, 0, k), 1, at_b(-1))

        def to_sibling(self, bs):
            self.side[bs] = move(unit(self.index, bs, 0, 0), unit(self.index, bs, 1, 0), 4, sibling)

        def start(self):
            if self.index:
                z_copies[self.index - 1].wait_recv()
            for k, step in ((1, 1), (2, -1), (3, 2)):
                self.a[k] = move(unit(self.index, 0, 0, 0), unit(self.index, 0, 0, k), 1, at_a(step))
            self.spread(0)

        def arrive_a(self):
            for k in (1, 2, 3):
                self.a[k].wait_recv()
                self.spread(k)
            self.to_sibling(0)

        def arrive_b(self):
            cut = UNIT // 2
            for k in range(4):
                here = unit(self.index, 3, 0, k)
                self.right[k].wait_recv()
                self.far.append(move(unit(self.index, 1, 0, k), here, 1, at_b(1), 0, UNIT - cut))
                self.left[k].wait_recv()
                self.far.append(move(unit(self.index, 2, 0, k), here, 1, at_b(-1), cut, 0))
            self.to_sibling(1)
            self.to_sibling(2)

        def arrive_far(self):
            for copy in self.far:
                copy.wait_recv()
            self.to_sibling(3)

        def arrive_side(self, *bss):
            for bs in bss:
                self.side[bs].wait_recv()

    streams = [Stream(i) for i in range(4)]
    streams[0].start()
    streams[1].start()
    streams[0].arrive_a()
    streams[2].start()
    streams[3].start()

    for copy in q_copies:
        copy.wait_recv()
    half = pl.ds(pl.multiple_of(core * 128, 128), 128)
    q_side = send(q_all.at[half, :], q_all.at[half, :], sibling)
    q_side.wait_recv()

    row_at = lax.broadcasted_iota(jnp.int32, (ROWS, 256), 0)
    col_at = lax.broadcasted_iota(jnp.int32, (ROWS, 256), 1)
    from_head = row_at // 4
    source = ((from_head % 2) * 8 + from_head // 2) * 16 + row_at % 4
    for part in range(4):
        pick = jnp.where(col_at == source + part * 4, 1.0, 0.0).astype(jnp.bfloat16)
        picked = dot(pick, q_all[...]).astype(jnp.bfloat16)
        q_own[:, part * 384 : part * 384 + 384] = picked[:, 0:384]
        draft[:, 128 + part * 128 : 256 + part * 128] = picked[:, 384:512]
        if part == 0:
            draft[:, 0:128] = picked[:, 512:640]
    q_peer_copy = send(q_own, q_peer, partner)

    lane = lax.broadcasted_iota(jnp.int32, (ROWS, 128), 1)

    def project(group, rows_ref):
        q_full[...] = dot(rows_ref[...], v_uq[...]).astype(jnp.bfloat16).astype(jnp.float32)
        cosine = jnp.concatenate([table_ref[0:8, :]] * 8, axis=0)
        sine = jnp.concatenate([table_ref[8:16, :]] * 8, axis=0)

        def absorb(h, nope, pe):
            rows = pl.ds(group * GROUP + h * ROWS, ROWS)
            turned = jnp.where(lane < 32, pltpu.roll(pe, 96, 1), pltpu.roll(pe, 32, 1))
            rotated = pe * cosine + turned * sine
            queries[rows, 0:128] = rotated.astype(jnp.bfloat16)
            queries[rows, 640:768] = pltpu.roll(rotated, 64, 1).astype(jnp.bfloat16)
            queries[rows, 128:640] = dot(nope.astype(jnp.bfloat16), v_uk[h]).astype(jnp.bfloat16)

        for pair in range(HEADS // 2):
            at = pair * 384
            middle = q_full[:, at + 128 : at + 256]
            end = pltpu.roll(q_full[:, at + 256 : at + 384], 64, 1)
            absorb(2 * pair, q_full[:, at : at + 128], middle)
            absorb(2 * pair + 1, jnp.where(lane < 64, pltpu.roll(middle, 64, 1), end), end)

    def score(rows, units):
        first, second = [], []
        low = [jnp.concatenate([keys[u * UNIT + t] for u in units], axis=0) for t in range(4)]
        high = [jnp.concatenate([keys[u * UNIT + 4 + t] for u in units], axis=0) for t in range(4)]
        rope = jnp.concatenate([keys[u * UNIT + 8] for u in units], axis=0)
        left = dot_t(queries[rows, 0:640], jnp.concatenate([rope] + low, axis=1))
        right = dot_t(queries[rows, 128:768], jnp.concatenate(high + [rope], axis=1))
        values = jnp.concatenate([jnp.concatenate(low, axis=1), jnp.concatenate(high, axis=1)], axis=0)
        return jnp.concatenate([left, right], axis=1) * SCALE, values

    def update(rows, scores, values, first=False):
        peak = jnp.max(scores, axis=1, keepdims=True)
        if first:
            new_top = jnp.broadcast_to(peak, (BLOCK, 128))
        else:
            old_top = top[rows, :]
            new_top = jnp.maximum(old_top, peak)
            factor = jnp.exp2(old_top - new_top)
        e = jnp.exp2(scores - new_top[:, 0:1])
        part = jnp.sum(e, axis=1, keepdims=True)
        summed = dot(e.astype(jnp.bfloat16), values)
        if first:
            total[rows, :] = jnp.broadcast_to(part, (BLOCK, 128))
            acc[rows, :] = summed
        else:
            total[rows, :] = total[rows, :] * factor + part
            acc[rows, :] = acc[rows, :] * factor[:, 0:1] + summed
        top[rows, :] = new_top

    def attend(items, done=None):
        held = None
        for group, block, units, first in items:
            rows = pl.ds(group * GROUP + block * BLOCK, BLOCK)
            now = (rows, *score(rows, units), first)
            if held is not None:
                update(*held)
                if done is not None:
                    done(0)
            held = now
        update(*held)
        if done is not None:
            done(1)

    def attend_draft():
        row = lax.broadcasted_iota(jnp.int32, (BLOCK, ROWS), 0) % ROWS
        col = lax.broadcasted_iota(jnp.int32, (BLOCK, ROWS), 1)
        begin = jnp.zeros((BLOCK, ROWS), jnp.int32)
        for i in range(8):
            begin = jnp.where(col // DRAFT == i, start_ref[i], begin)
        seen = (row // DRAFT == col // DRAFT) & (col % DRAFT <= row % DRAFT) & (begin <= col % DRAFT)
        bias = jnp.where(seen, 0.0, -1e30)
        for block in range(2):
            rows = pl.ds(block * BLOCK, BLOCK)
            scores = dot_t(queries[rows, 0:640], draft[...]) * SCALE + bias
            update(rows, scores, draft[:, 128:640], True)

    def context(group, h):
        rows = pl.ds(group * GROUP + h * ROWS, ROWS)
        ctx = (acc[rows, :] * (1.0 / total[rows, 0:1])).astype(jnp.bfloat16)
        return dot(ctx, v_uv[h]), top[rows, :] + jnp.log2(total[rows, :])

    def pair(group, units, first=False):
        return [(group, 0, units, first), (group, 1, units, first)]

    weights[0].wait()
    weights[1].wait()
    project(0, q_own)
    streams[1].arrive_a()
    attend_draft()
    streams[2].arrive_a()
    streams[0].arrive_side(0)
    streams[1].arrive_side(0)
    attend(pair(0, chunk((0, 1), (0,))))
    streams[3].arrive_a()
    streams[0].arrive_b()
    q_peer_copy.wait_recv()
    project(1, q_peer)
    streams[1].arrive_b()
    streams[2].arrive_side(0)
    streams[3].arrive_side(0)
    attend(pair(1, chunk((0, 1, 2, 3), (0,)), True))
    streams[2].arrive_b()
    streams[3].arrive_b()
    attend(pair(0, chunk((2, 3), (0,))))
    streams[0].arrive_side(1, 2)
    streams[1].arrive_side(1, 2)
    attend(pair(1, chunk((0, 1), (1, 2))))
    streams[0].arrive_far()
    streams[1].arrive_far()
    streams[2].arrive_side(1, 2)
    streams[3].arrive_side(1, 2)
    attend(pair(1, chunk((2, 3), (1, 2))))
    streams[2].arrive_far()
    streams[3].arrive_far()
    streams[0].arrive_side(3)
    streams[1].arrive_side(3)
    attend(pair(1, chunk((0, 1), (3,))))
    streams[2].arrive_side(3)
    streams[3].arrive_side(3)
    weights[2].wait()
    o_copies = []

    def hand_over(part):
        shares = s_send[...] if part else jnp.zeros((ROWS, 128), jnp.float32)
        for i in range(HEADS // 2):
            h = part * (HEADS // 2) + i
            value, share = context(1, h)
            o_send[part, :, i * VD : i * VD + VD] = value.astype(jnp.bfloat16)
            shares = jnp.where(lane == h, share, shares)
        s_send[...] = shares
        o_copies.append(send(o_send.at[part], o_recv.at[part], partner))
        if part:
            o_copies.append(send(s_send, s_recv, partner))

    attend(pair(1, chunk((2, 3), (3,))), hand_over)
    attend(
        pair(0, chunk((0, 1), (1, 2))) + pair(0, chunk((2, 3), (1, 2))) + pair(0, chunk((0, 1, 2, 3), (3,)))
    )
    own = [context(0, h) for h in range(HEADS)]
    for copy in o_copies:
        copy.wait_recv()
    for h, (value, share) in enumerate(own):
        other = jnp.broadcast_to(s_recv[:, h : h + 1], (ROWS, 128))
        mine = 1.0 / (1.0 + jnp.exp2(jnp.minimum(other - share, 120.0)))
        theirs = 1.0 / (1.0 + jnp.exp2(jnp.minimum(share - other, 120.0)))
        part, at = h // 4, (h % 4) * VD
        peer = o_recv[part, :, at : at + VD].astype(jnp.float32)
        out_ref[:, h * VD : h * VD + VD] = (value * mine + peer * theirs).astype(jnp.bfloat16)
    for copy in sent:
        copy.wait_send()


def on_device(
    q_latent, draft_latent, draft_rope, draft_start, prompt_latent, prompt_rope, w_uq, w_uk, w_uv
):
    vmem = pl.BlockSpec(memory_space=pltpu.VMEM)
    hbm = pl.BlockSpec(memory_space=pltpu.HBM)
    bf16, f32 = jnp.bfloat16, jnp.float32
    return pl.pallas_call(
        kernel,
        name="attention",
        out_shape=jax.ShapeDtypeStruct((ROWS, HEADS * VD), bf16),
        in_specs=[hbm] * 10,
        out_specs=vmem,
        scratch_shapes=[
            pltpu.VMEM((4, QLORA), bf16),
            pltpu.VMEM((4, KVL), bf16),
            pltpu.VMEM((4, ROPE), bf16),
            pltpu.SMEM((8,), jnp.int32),
            pltpu.VMEM((32, KVL), bf16),
            pltpu.VMEM((32, ROPE), bf16),
            pltpu.VMEM((16, 128), f32),
            pltpu.VMEM((UNITS * UNIT, 16, 128), bf16),
            pltpu.VMEM((16, 640), bf16),
            pltpu.VMEM((256, 640), bf16),
            pltpu.VMEM((16, 640), f32),
            pltpu.VMEM((ROWS, QLORA), bf16),
            pltpu.VMEM((ROWS, QLORA), bf16),
            pltpu.VMEM((ROWS, QLORA), f32),
            pltpu.VMEM((2 * GROUP, 768), bf16),
            pltpu.VMEM((ROWS, 640), bf16),
            pltpu.VMEM((2 * GROUP, KVL), f32),
            pltpu.VMEM((2 * GROUP, 128), f32),
            pltpu.VMEM((2 * GROUP, 128), f32),
            pltpu.VMEM((2, ROWS, HEADS * VD // 2), bf16),
            pltpu.VMEM((2, ROWS, HEADS * VD // 2), bf16),
            pltpu.VMEM((ROWS, 128), f32),
            pltpu.VMEM((ROWS, 128), f32),
            pltpu.VMEM((QLORA, HEADS * (NOPE + ROPE)), bf16),
            pltpu.VMEM((HEADS, NOPE, KVL), bf16),
            pltpu.VMEM((HEADS, KVL, VD), bf16),
            pltpu.SemaphoreType.DMA((10,)),
            pltpu.SemaphoreType.DMA((112,)),
            pltpu.SemaphoreType.DMA((112,)),
        ],
        compiler_params=pltpu.CompilerParams(
            collective_id=0, has_side_effects=True, vmem_limit_bytes=64 * 2**20
        ),
    )(
        q_latent, draft_latent, draft_rope, draft_start, prompt_latent, prompt_rope,
        rotation_table(), w_uq, w_uk, w_uv,
    )


def solution(mesh):
    in_specs = (
        P(("grp", "head"), None),
        P(("grp", "head"), None),
        P(("grp", "head"), None),
        P("grp"),
        P(("grp", "head"), None),
        P(("grp", "head"), None),
        P(None, "head"),
        P("head", None, None),
        P("head", None, None),
    )
    out_specs = P("grp", "head")
    return jax.shard_map(
        on_device, mesh=mesh, in_specs=in_specs, out_specs=out_specs, check_vma=False
    )
```

```python
import math

import jax
import jax.numpy as jnp
import numpy as np
from jax import lax
from jax.experimental import pallas as pl
from jax.experimental.pallas import tpu as pltpu
from jax.sharding import PartitionSpec as P

MESH = pl.DeviceIdType.MESH
KVL = 512
ROPE = 64
NOPE = 128
VD = 128
DRAFT = 8
PROMPT = 8192
QLORA = 1536
ROWS = 64
HEADS = 8
GROUP = ROWS * HEADS
SCALE = math.log2(math.e) / math.sqrt(NOPE + ROPE)
UNIT = 9
UNITS = 128
BLOCK = 256
NT = (((1,), (1,)), ((), ()))


def rotation_table():
    half = ROPE // 2
    freq = np.float32(10000.0) ** (-np.arange(half, dtype=np.float32) / np.float32(half))
    position = PROMPT + np.arange(DRAFT, dtype=np.float32)
    angle = (position[:, None] * freq[None, :].astype(np.float32)).astype(np.float64)
    zero = np.zeros((DRAFT, 2 * half))
    cosine = np.concatenate([np.cos(angle), np.cos(angle), zero], axis=1)
    sine = np.concatenate([-np.sin(angle), np.sin(angle), zero], axis=1)
    return np.concatenate([cosine, sine], axis=0).astype(np.float32)


def unit(stream, bs, cs, as_):
    return ((stream * 4 + bs) * 2 + cs) * 4 + as_


def chunk(streams, bss):
    return [unit(s, b, c, a) for s in streams for b in bss for c in (0, 1) for a in range(4)]


def dot_t(a, b):
    return lax.dot_general(a, b, NT, preferred_element_type=jnp.float32)


def dot(a, b):
    return jnp.dot(a, b, preferred_element_type=jnp.float32)


def kernel(
    ql_in, dl_in, dr_in, start_in, pl_in, pr_in, table_in, w_uq, w_uk, w_uv, out_ref,
    ql_ref, dl_ref, dr_ref, start_ref, pl_ref, pr_ref, table_ref,
    keys, q_send, q_all, d_send, d_all, q_stage, q_rows, q_full, queries, draft, draft_bias, acc, top, total,
    o_send, o_recv, s_send, s_recv, shares, v_uq, v_uk, v_uv, local_sem, send_sem, recv_sem,
):
    grp, head = lax.axis_index("grp"), lax.axis_index("head")
    x, y, z, core = head // 4, (grp // 8) * 2 + (head // 2) % 2, grp % 8, head % 2
    toward = 2 * (z % 2) - 1

    def place(px, py, pz, pc):
        return ((py // 2) * 8 + pz, px * 4 + (py % 2) * 2 + pc)

    def at_a(step):
        return place((x + step * core + 4) % 4, (y + step * (1 - core) + 4) % 4, z, core)

    def at_b(step):
        return place((x + step * (1 - core) + 4) % 4, (y + step * core + 4) % 4, z, core)

    def at_z(step):
        return place(x, y, (z + step + 8) % 8, core)

    beside = y + 1 - 2 * (y % 2)
    sibling = place(x, y, z, 1 - core)
    partner = at_z(-toward)
    beyond = (z - toward + 8) % 8
    near = [place((x + dx) % 4, y, z, core) for dx in (1, 3, 2)]
    near += [place((x + dx) % 4, beside, z, core) for dx in (0, 1, 3, 2)]
    across = [place((x + dx) % 4, py, beyond, core) for py in (y, beside) for dx in (0, 1, 3, 2)]
    greeted = near + across + [place(x, (y + 3 + 2 * (y % 2)) % 4, z, core), place(x, (y + 2) % 4, z, core)]
    greeted += [at_z(toward), at_z(3 * toward), at_z(2), at_z(-2), sibling]

    loads = [
        pltpu.make_async_copy(src, dst, local_sem.at[i])
        for i, (src, dst) in enumerate((
            (pl_in, pl_ref), (pr_in, pr_ref), (ql_in, ql_ref), (dl_in, dl_ref), (dr_in, dr_ref),
            (table_in, table_ref), (start_in, start_ref), (w_uq, v_uq), (w_uk, v_uk), (w_uv, v_uv),
        ))
    ]
    inputs, weights = loads[:7], loads[7:]
    for copy in inputs:
        copy.start()
    barrier = pltpu.get_barrier_semaphore()
    for device in greeted:
        pl.semaphore_signal(barrier, inc=1, device_id=device, device_id_type=MESH)
    for copy in weights:
        copy.start()
    for copy in inputs:
        copy.wait()

    def send(src, dst, device, left, landed):
        pltpu.make_async_remote_copy(
            src_ref=src, dst_ref=dst, send_sem=send_sem.at[left], recv_sem=recv_sem.at[landed],
            device_id=device, device_id_type=MESH,
        ).start()

    def arrived(landed, ref):
        pltpu.make_async_copy(ref, ref, recv_sem.at[landed]).wait()

    def gone(left, ref):
        pltpu.make_async_copy(ref, ref, send_sem.at[left]).wait()

    def tiles(at, count=1, first=0, last=0):
        return keys.at[pl.ds(at * UNIT + first, count * UNIT - first - last)]

    def move(src, dst, count, device, landed, first=0, last=0):
        send(tiles(src, count, first, last), tiles(dst, count, first, last), device, 0, landed)

    for row in range(2):
        for lane in range(4):
            keys[row * 4 + lane] = pl_ref[row * 16 : row * 16 + 16, lane * 128 : lane * 128 + 128]
    keys[8] = jnp.concatenate([pr_ref[0:16, :], pr_ref[16:32, :]], axis=1)
    q_stage[...] = jnp.zeros(q_stage.shape, jnp.float32)
    for part in range(4):
        q_stage[part * 4 : part * 4 + 4, 0:384] = ql_ref[:, part * 384 : part * 384 + 384].astype(jnp.float32)
        q_stage[part * 4 : part * 4 + 4, 384:512] = dl_ref[:, part * 128 : part * 128 + 128].astype(jnp.float32)
    q_stage[0:4, 512:576] = dr_ref[...].astype(jnp.float32)
    q_send[...] = q_stage[:, 0:384].astype(jnp.bfloat16)
    d_send[...] = q_stage[:, 384:640].astype(jnp.bfloat16)

    def slot(base):
        return pl.ds(pl.multiple_of(base + head // 2 * 16, 16), 16)

    q_all[slot(core * 256), :] = q_send[...]
    d_all[slot(core * 128), :] = d_send[...]

    pl.semaphore_wait(barrier, len(greeted))

    for device in near:
        send(q_send, q_all.at[slot(core * 256), :], device, 1, 0)
    for device in across:
        send(q_send, q_all.at[slot(core * 256 + 128), :], device, 1, 0)
    for stream, step in ((1, toward), (2, -2 * toward), (3, 3 * toward)):
        move(unit(0, 0, 0, 0), unit(stream, 0, 0, 0), 1, at_z(step), 8 + stream)

    class Stream:
        def __init__(self, index):
            self.index = index
            self.sem = 12 + index * 6

        def spread(self, k):
            own = unit(self.index, 0, 0, k)
            move(own, unit(self.index, 1, 0, k), 1, at_b(1), self.sem + 1)
            move(own, unit(self.index, 2, 0, k), 1, at_b(-1), self.sem + 1)

        def to_sibling(self, bs, count=1):
            sem = self.sem + 3 + (bs + 1) // 2
            for i in range(bs, bs + count):
                move(unit(self.index, i, 0, 0), unit(self.index, i, 1, 0), 4, sibling, sem)

        def start(self):
            if self.index:
                arrived(8 + self.index, tiles(0))
            for k, step in ((1, 1), (2, -1), (3, 2)):
                move(unit(self.index, 0, 0, 0), unit(self.index, 0, 0, k), 1, at_a(step), self.sem)
            self.spread(0)

        def arrive_a(self):
            arrived(self.sem, tiles(0, 3))
            for k in (1, 2, 3):
                self.spread(k)
            self.to_sibling(0)

        def arrive_b(self):
            cut = UNIT // 2
            arrived(self.sem + 1, tiles(0, 8))
            for k in range(4):
                here = unit(self.index, 3, 0, k)
                move(unit(self.index, 1, 0, k), here, 1, at_b(1), self.sem + 2, 0, UNIT - cut)
                move(unit(self.index, 2, 0, k), here, 1, at_b(-1), self.sem + 2, cut, 0)
            self.to_sibling(1, 2)

        def arrive_far(self):
            arrived(self.sem + 2, tiles(0, 4))
            self.to_sibling(3)

        def arrive_side(self, bs):
            arrived(self.sem + 3 + (bs + 1) // 2, tiles(0, 8 if bs == 1 else 4))

    streams = [Stream(i) for i in range(4)]
    streams[0].start()
    streams[1].start()
    for device in near:
        send(d_send, d_all.at[slot(core * 128), :], device, 2, 1)
    streams[0].arrive_a()
    arrived(0, q_all.at[0:240, :])
    q_half = pl.ds(pl.multiple_of(core * 256, 256), 256)
    send(q_all.at[q_half, :], q_all.at[q_half, :], sibling, 3, 2)
    streams[2].start()
    streams[3].start()
    d_half = pl.ds(pl.multiple_of(core * 128, 128), 128)
    arrived(2, q_all.at[0:256, :])

    row_at = lax.broadcasted_iota(jnp.int32, (ROWS, 256), 0)
    col_at = lax.broadcasted_iota(jnp.int32, (ROWS, 256), 1)
    from_head = row_at // 4
    source = ((from_head % 2) * 8 + from_head // 2) * 16 + row_at % 4
    picks = [
        jnp.where(col_at == source + part * 4, 1.0, 0.0).astype(jnp.bfloat16) for part in range(4)
    ]
    for group in range(2):
        mixed = jnp.concatenate([q_all[i + group * 128 : i + group * 128 + 128, :] for i in (0, 256)], axis=0)
        for part in range(4):
            q_rows[group * ROWS : group * ROWS + ROWS, part * 384 : part * 384 + 384] = dot(
                picks[part], mixed
            ).astype(jnp.bfloat16)

    lane = lax.broadcasted_iota(jnp.int32, (ROWS, 128), 1)
    wide = lax.broadcasted_iota(jnp.int32, (2 * ROWS, 128), 1)

    def project():
        q_full[...] = dot(q_rows[...], v_uq[...]).astype(jnp.bfloat16).astype(jnp.float32)

    def absorb_all():
        cosine = jnp.concatenate([table_ref[0:8, :]] * 16, axis=0)
        sine = jnp.concatenate([table_ref[8:16, :]] * 16, axis=0)

        def absorb(h, nope, pe):
            turned = jnp.where(wide < 32, pltpu.roll(pe, 96, 1), pltpu.roll(pe, 32, 1))
            rotated = pe * cosine + turned * sine
            first = rotated.astype(jnp.bfloat16)
            second = pltpu.roll(rotated, 64, 1).astype(jnp.bfloat16)
            absorbed = dot(nope.astype(jnp.bfloat16), v_uk[h]).astype(jnp.bfloat16)
            for group in range(2):
                rows = pl.ds(group * GROUP + h * ROWS, ROWS)
                part = slice(group * ROWS, group * ROWS + ROWS)
                queries[rows, 0:128] = first[part]
                queries[rows, 640:768] = second[part]
                queries[rows, 128:640] = absorbed[part]

        for two in range(HEADS // 2):
            at = two * 384
            middle = q_full[:, at + 128 : at + 256]
            end = pltpu.roll(q_full[:, at + 256 : at + 384], 64, 1)
            absorb(2 * two, q_full[:, at : at + 128], middle)
            absorb(2 * two + 1, jnp.where(wide < 64, pltpu.roll(middle, 64, 1), end), end)

    def score(rows, units, with_draft=False):
        low = [jnp.concatenate([keys[u * UNIT + t] for u in units], axis=0) for t in range(4)]
        high = [jnp.concatenate([keys[u * UNIT + 4 + t] for u in units], axis=0) for t in range(4)]
        rope = jnp.concatenate([keys[u * UNIT + 8] for u in units], axis=0)
        left = dot_t(queries[rows, 0:640], jnp.concatenate([rope] + low, axis=1))
        right = dot_t(queries[rows, 128:768], jnp.concatenate(high + [rope], axis=1))
        values = [jnp.concatenate(low, axis=1), jnp.concatenate(high, axis=1)]
        scores = [left * SCALE, right * SCALE]
        if with_draft:
            bias = jnp.concatenate([draft_bias[...]] * (BLOCK // ROWS), axis=0)
            scores.append(dot_t(queries[rows, 0:640], draft[...]) * SCALE + bias)
            values.append(draft[:, 128:640])
        return jnp.concatenate(scores, axis=1), jnp.concatenate(values, axis=0)

    def update(rows, scores, values, first=False):
        peak = jnp.max(scores, axis=1, keepdims=True)
        if first:
            new_top = jnp.broadcast_to(peak, (BLOCK, 128))
        else:
            old_top = top[rows, :]
            new_top = jnp.maximum(old_top, peak)
            factor = jnp.exp2(old_top - new_top)
        e = jnp.exp2(scores - new_top[:, 0:1])
        part = jnp.sum(e, axis=1, keepdims=True)
        summed = dot(e.astype(jnp.bfloat16), values)
        if first:
            total[rows, :] = jnp.broadcast_to(part, (BLOCK, 128))
            acc[rows, :] = summed
        else:
            total[rows, :] = total[rows, :] * factor + part
            acc[rows, :] = acc[rows, :] * factor[:, 0:1] + summed
        top[rows, :] = new_top

    held = []

    def settle():
        if held:
            update(*held.pop())

    def attend(items):
        for group, block, units, first, with_draft in items:
            rows = pl.ds(group * GROUP + block * BLOCK, BLOCK)
            now = (rows, *score(rows, units, with_draft), first)
            settle()
            held.append(now)

    def gather_draft():
        draft[ROWS:128, :] = jnp.zeros((128 - ROWS, 640), jnp.bfloat16)
        for part in range(4):
            picked = dot(picks[part], d_all[...]).astype(jnp.bfloat16)
            draft[0:ROWS, 128 + part * 128 : 256 + part * 128] = picked[:, 0:128]
            if part == 0:
                draft[0:ROWS, 0:128] = picked[:, 128:256]
        row = lax.broadcasted_iota(jnp.int32, (ROWS, 128), 0)
        col = lax.broadcasted_iota(jnp.int32, (ROWS, 128), 1)
        begin = jnp.zeros((ROWS, 128), jnp.int32)
        for i in range(8):
            begin = jnp.where((col >> 3) == i, start_ref[i], begin)
        seen = ((row >> 3) == (col >> 3)) & (col <= row) & (begin <= (col & 7))
        draft_bias[...] = jnp.where(seen, 0.0, -1e30)

    def context(group, h):
        rows = pl.ds(group * GROUP + h * ROWS, ROWS)
        ctx = (acc[rows, :] * (1.0 / total[rows, 0:1])).astype(jnp.bfloat16)
        return dot(ctx, v_uv[h]), top[rows, :] + jnp.log2(total[rows, :])

    def pair(group, units, first=False, with_draft=False):
        return [(group, block, units, first, with_draft) for block in range(2)]

    weights[0].wait()
    weights[1].wait()
    project()
    streams[1].arrive_a()
    absorb_all()
    streams[0].arrive_side(0)
    streams[1].arrive_side(0)
    attend(pair(1, chunk((0, 1), (0,)), True))
    streams[2].arrive_a()
    arrived(1, d_all.at[0:112, :])
    send(d_all.at[d_half, :], d_all.at[d_half, :], sibling, 4, 3)
    attend(pair(0, chunk((0, 1), (0,)), True))
    streams[3].arrive_a()
    streams[0].arrive_b()
    streams[2].arrive_side(0)
    streams[3].arrive_side(0)
    attend(pair(1, chunk((2, 3), (0,))))
    streams[1].arrive_b()
    attend(pair(0, chunk((2, 3), (0,))))
    streams[2].arrive_b()
    streams[0].arrive_side(1)
    streams[1].arrive_side(1)
    attend(pair(1, chunk((0, 1), (1, 2))))
    streams[3].arrive_b()
    arrived(3, d_all.at[0:128, :])
    gather_draft()
    attend(pair(0, chunk((0, 1), (1, 2))))
    streams[0].arrive_far()
    streams[1].arrive_far()
    streams[2].arrive_side(1)
    streams[3].arrive_side(1)
    attend(pair(1, chunk((2, 3), (1, 2))))
    streams[2].arrive_far()
    streams[3].arrive_far()
    streams[0].arrive_side(3)
    streams[1].arrive_side(3)
    attend(pair(1, chunk((0, 1), (3,))))
    streams[2].arrive_side(3)
    streams[3].arrive_side(3)
    weights[2].wait()
    def hand_over(part):
        if part == 0:
            shares[...] = jnp.zeros((128, 128), jnp.float32)
        for i in range(HEADS // 2):
            h = part * (HEADS // 2) + i
            value, share = context(1, h)
            o_send[part, :, i * VD : i * VD + VD] = value.astype(jnp.bfloat16)
            shares[0:ROWS, :] = jnp.where(lane == h, share, shares[0:ROWS, :])
        send(o_send.at[part], o_recv.at[part], partner, 5, 4)
        if part:
            s_send[...] = jnp.transpose(shares[...])[0:HEADS, :]
            send(s_send, s_recv, partner, 6, 5)

    attend(pair(1, chunk((2, 3), (3,))))
    hand_over(0)
    rest = pair(0, chunk((2, 3), (1, 2)), False, True) + pair(0, chunk((0, 1, 2, 3), (3,)))
    attend(rest[:1])
    hand_over(1)
    attend(rest[1:])
    settle()
    own = []

    def finish():
        own.extend(context(0, h) for h in range(HEADS))

    def collect():
        arrived(4, o_recv)
        arrived(5, s_recv)

    def merge():
        shares[0:HEADS, :] = s_recv[...]
        others = jnp.transpose(shares[...])
        for h, (value, share) in enumerate(own):
            other = jnp.broadcast_to(others[0:ROWS, h : h + 1], (ROWS, 128))
            mine = 1.0 / (1.0 + jnp.exp2(jnp.minimum(other - share, 120.0)))
            theirs = 1.0 / (1.0 + jnp.exp2(jnp.minimum(share - other, 120.0)))
            part, at = h // 4, (h % 4) * VD
            peer = o_recv[part, :, at : at + VD].astype(jnp.float32)
            out_ref[:, h * VD : h * VD + VD] = (value * mine + peer * theirs).astype(jnp.bfloat16)

    def drain():
        gone(0, tiles(0, 127))
        gone(1, q_all.at[0:240, :])
        gone(2, d_all.at[0:112, :])
        gone(3, q_all.at[0:256, :])
        gone(4, d_all.at[0:128, :])
        gone(5, o_send)
        gone(6, s_send)

    finish()
    collect()
    merge()
    drain()


def on_device(
    q_latent, draft_latent, draft_rope, draft_start, prompt_latent, prompt_rope, w_uq, w_uk, w_uv
):
    vmem = pl.BlockSpec(memory_space=pltpu.VMEM)
    hbm = pl.BlockSpec(memory_space=pltpu.HBM)
    bf16, f32 = jnp.bfloat16, jnp.float32
    return pl.pallas_call(
        kernel,
        name="attention",
        out_shape=jax.ShapeDtypeStruct((ROWS, HEADS * VD), bf16),
        in_specs=[hbm] * 10,
        out_specs=vmem,
        scratch_shapes=[
            pltpu.VMEM((4, QLORA), bf16),
            pltpu.VMEM((4, KVL), bf16),
            pltpu.VMEM((4, ROPE), bf16),
            pltpu.SMEM((8,), jnp.int32),
            pltpu.VMEM((32, KVL), bf16),
            pltpu.VMEM((32, ROPE), bf16),
            pltpu.VMEM((16, 128), f32),
            pltpu.VMEM((UNITS * UNIT, 16, 128), bf16),
            pltpu.VMEM((16, 384), bf16),
            pltpu.VMEM((512, 384), bf16),
            pltpu.VMEM((16, 256), bf16),
            pltpu.VMEM((256, 256), bf16),
            pltpu.VMEM((16, 640), f32),
            pltpu.VMEM((2 * ROWS, QLORA), bf16),
            pltpu.VMEM((2 * ROWS, QLORA), f32),
            pltpu.VMEM((2 * GROUP, 768), bf16),
            pltpu.VMEM((128, 640), bf16),
            pltpu.VMEM((ROWS, 128), f32),
            pltpu.VMEM((2 * GROUP, KVL), f32),
            pltpu.VMEM((2 * GROUP, 128), f32),
            pltpu.VMEM((2 * GROUP, 128), f32),
            pltpu.VMEM((2, ROWS, HEADS * VD // 2), bf16),
            pltpu.VMEM((2, ROWS, HEADS * VD // 2), bf16),
            pltpu.VMEM((HEADS, 128), f32),
            pltpu.VMEM((HEADS, 128), f32),
            pltpu.VMEM((128, 128), f32),
            pltpu.VMEM((QLORA, HEADS * (NOPE + ROPE)), bf16),
            pltpu.VMEM((HEADS, NOPE, KVL), bf16),
            pltpu.VMEM((HEADS, KVL, VD), bf16),
            pltpu.SemaphoreType.DMA((10,)),
            pltpu.SemaphoreType.DMA((7,)),
            pltpu.SemaphoreType.DMA((36,)),
        ],
        compiler_params=pltpu.CompilerParams(
            collective_id=0, has_side_effects=True, vmem_limit_bytes=64 * 2**20
        ),
    )(
        q_latent, draft_latent, draft_rope, draft_start, prompt_latent, prompt_rope,
        rotation_table(), w_uq, w_uk, w_uv,
    )


def solution(mesh):
    in_specs = (
        P(("grp", "head"), None),
        P(("grp", "head"), None),
        P(("grp", "head"), None),
        P("grp"),
        P(("grp", "head"), None),
        P(("grp", "head"), None),
        P(None, "head"),
        P("head", None, None),
        P("head", None, None),
    )
    out_specs = P("grp", "head")
    return jax.shard_map(
        on_device, mesh=mesh, in_specs=in_specs, out_specs=out_specs, check_vma=False
    )
```

```python
import math

import jax
import jax.numpy as jnp
import numpy as np
from jax import lax
from jax.experimental import pallas as pl
from jax.experimental.pallas import tpu as pltpu
from jax.sharding import PartitionSpec as P

MESH = pl.DeviceIdType.MESH
KVL = 512
ROPE = 64
NOPE = 128
VD = 128
DRAFT = 8
PROMPT = 8192
QLORA = 1536
ROWS = 64
HEADS = 8
GROUP = ROWS * HEADS
SCALE = math.log2(math.e) / math.sqrt(NOPE + ROPE)
UNIT = 9
UNITS = 128
BLOCK = 256
NT = (((1,), (1,)), ((), ()))


def rotation_table():
    half = ROPE // 2
    freq = np.float32(10000.0) ** (-np.arange(half, dtype=np.float32) / np.float32(half))
    position = PROMPT + np.arange(DRAFT, dtype=np.float32)
    angle = (position[:, None] * freq[None, :].astype(np.float32)).astype(np.float64)
    zero = np.zeros((DRAFT, 2 * half))
    cosine = np.concatenate([np.cos(angle), np.cos(angle), zero], axis=1)
    sine = np.concatenate([-np.sin(angle), np.sin(angle), zero], axis=1)
    return np.concatenate([cosine, sine], axis=0).astype(np.float32)


def unit(stream, bs, cs, as_):
    return ((stream * 4 + bs) * 2 + cs) * 4 + as_


def chunk(streams, bss):
    return [unit(s, b, c, a) for s in streams for b in bss for c in (0, 1) for a in range(4)]


def dot_t(a, b):
    return lax.dot_general(a, b, NT, preferred_element_type=jnp.float32)


def dot(a, b):
    return jnp.dot(a, b, preferred_element_type=jnp.float32)


def kernel(
    ql_in, dl_in, dr_in, start_in, pl_in, pr_in, table_in, w_uq, w_uk, w_uv, out_ref,
    ql_ref, dl_ref, dr_ref, start_ref, pl_ref, pr_ref, table_ref,
    keys, q_send, q_all, d_send, d_all, q_stage, q_rows, q_full, queries, draft, draft_bias, acc, top, total,
    o_send, o_recv, s_send, s_recv, shares, v_uq, v_uk, v_uv, local_sem, send_sem, recv_sem,
):
    grp, head = lax.axis_index("grp"), lax.axis_index("head")
    x, y, z, core = head // 4, (grp // 8) * 2 + (head // 2) % 2, grp % 8, head % 2
    toward = 2 * (z % 2) - 1

    def place(px, py, pz, pc):
        return ((py // 2) * 8 + pz, px * 4 + (py % 2) * 2 + pc)

    def at_a(step):
        return place((x + step * core + 4) % 4, (y + step * (1 - core) + 4) % 4, z, core)

    def at_b(step):
        return place((x + step * (1 - core) + 4) % 4, (y + step * core + 4) % 4, z, core)

    def at_z(step):
        return place(x, y, (z + step + 8) % 8, core)

    beside = y + 1 - 2 * (y % 2)
    sibling = place(x, y, z, 1 - core)
    partner = at_z(-toward)
    beyond = (z - toward + 8) % 8
    near = [place((x + dx) % 4, y, z, core) for dx in (1, 3, 2)]
    near += [place((x + dx) % 4, beside, z, core) for dx in (0, 1, 3, 2)]
    across = [place((x + dx) % 4, py, beyond, core) for py in (y, beside) for dx in (0, 1, 3, 2)]
    greeted = near + across + [place(x, (y + 3 + 2 * (y % 2)) % 4, z, core), place(x, (y + 2) % 4, z, core)]
    greeted += [at_z(toward), at_z(3 * toward), at_z(2), at_z(-2), sibling]

    barrier = pltpu.get_barrier_semaphore()
    for device in greeted:
        pl.semaphore_signal(barrier, inc=1, device_id=device, device_id_type=MESH)
    loads = [
        pltpu.make_async_copy(src, dst, local_sem.at[i])
        for i, (src, dst) in enumerate((
            (pl_in, pl_ref), (pr_in, pr_ref), (ql_in, ql_ref), (dl_in, dl_ref), (dr_in, dr_ref),
            (table_in, table_ref), (start_in, start_ref), (w_uq, v_uq), (w_uk, v_uk), (w_uv, v_uv),
        ))
    ]
    inputs, weights = loads[:7], loads[7:]
    for copy in inputs:
        copy.start()
    for copy in weights:
        copy.start()
    for copy in inputs:
        copy.wait()

    def send(src, dst, device, left, landed):
        pltpu.make_async_remote_copy(
            src_ref=src, dst_ref=dst, send_sem=send_sem.at[left], recv_sem=recv_sem.at[landed],
            device_id=device, device_id_type=MESH,
        ).start()

    def arrived(landed, ref):
        pltpu.make_async_copy(ref, ref, recv_sem.at[landed]).wait()

    def gone(left, ref):
        pltpu.make_async_copy(ref, ref, send_sem.at[left]).wait()

    def tiles(at, count=1, first=0, last=0):
        return keys.at[pl.ds(at * UNIT + first, count * UNIT - first - last)]

    def move(src, dst, count, device, landed, first=0, last=0):
        send(tiles(src, count, first, last), tiles(dst, count, first, last), device, 0, landed)

    for row in range(2):
        for lane in range(4):
            keys[row * 4 + lane] = pl_ref[row * 16 : row * 16 + 16, lane * 128 : lane * 128 + 128]
    keys[8] = jnp.concatenate([pr_ref[0:16, :], pr_ref[16:32, :]], axis=1)
    q_stage[...] = jnp.zeros(q_stage.shape, jnp.float32)
    for part in range(4):
        q_stage[part * 4 : part * 4 + 4, 0:384] = ql_ref[:, part * 384 : part * 384 + 384].astype(jnp.float32)
        q_stage[part * 4 : part * 4 + 4, 384:512] = dl_ref[:, part * 128 : part * 128 + 128].astype(jnp.float32)
    q_stage[0:4, 512:576] = dr_ref[...].astype(jnp.float32)
    q_send[...] = q_stage[:, 0:384].astype(jnp.bfloat16)
    d_send[...] = q_stage[:, 384:640].astype(jnp.bfloat16)

    def slot(base):
        return pl.ds(pl.multiple_of(base + head // 2 * 16, 16), 16)

    q_all[slot(core * 256), :] = q_send[...]
    d_all[slot(core * 128), :] = d_send[...]

    pl.semaphore_wait(barrier, len(greeted))

    for device in near:
        send(q_send, q_all.at[slot(core * 256), :], device, 1, 0)
    for device in across:
        send(q_send, q_all.at[slot(core * 256 + 128), :], device, 1, 0)
    for stream, step in ((1, toward), (2, -2 * toward), (3, 3 * toward)):
        move(unit(0, 0, 0, 0), unit(stream, 0, 0, 0), 1, at_z(step), 8 + stream)

    class Stream:
        def __init__(self, index):
            self.index = index
            self.sem = 12 + index * 6

        def spread(self, k):
            own = unit(self.index, 0, 0, k)
            move(own, unit(self.index, 1, 0, k), 1, at_b(1), self.sem + 1)
            move(own, unit(self.index, 2, 0, k), 1, at_b(-1), self.sem + 1)

        def to_sibling(self, bs, count=1):
            sem = self.sem + 3 + (bs + 1) // 2
            for i in range(bs, bs + count):
                move(unit(self.index, i, 0, 0), unit(self.index, i, 1, 0), 4, sibling, sem)

        def start(self):
            if self.index:
                arrived(8 + self.index, tiles(0))
            for k, step in ((1, 1), (2, -1), (3, 2)):
                move(unit(self.index, 0, 0, 0), unit(self.index, 0, 0, k), 1, at_a(step), self.sem)
            self.spread(0)

        def arrive_a(self):
            arrived(self.sem, tiles(0, 3))
            for k in (1, 2, 3):
                self.spread(k)
            self.to_sibling(0)

        def arrive_b(self):
            cut = UNIT // 2
            arrived(self.sem + 1, tiles(0, 8))
            for k in range(4):
                here = unit(self.index, 3, 0, k)
                move(unit(self.index, 1, 0, k), here, 1, at_b(1), self.sem + 2, 0, UNIT - cut)
                move(unit(self.index, 2, 0, k), here, 1, at_b(-1), self.sem + 2, cut, 0)
            self.to_sibling(1, 2)

        def arrive_far(self):
            arrived(self.sem + 2, tiles(0, 4))
            self.to_sibling(3)

        def arrive_side(self, bs):
            arrived(self.sem + 3 + (bs + 1) // 2, tiles(0, 8 if bs == 1 else 4))

    streams = [Stream(i) for i in range(4)]
    streams[0].start()
    streams[1].start()
    for device in near:
        send(d_send, d_all.at[slot(core * 128), :], device, 2, 1)
    streams[0].arrive_a()
    arrived(0, q_all.at[0:240, :])
    q_half = pl.ds(pl.multiple_of(core * 256, 256), 256)
    send(q_all.at[q_half, :], q_all.at[q_half, :], sibling, 3, 2)
    streams[2].start()
    streams[3].start()
    d_half = pl.ds(pl.multiple_of(core * 128, 128), 128)

    row_at = lax.broadcasted_iota(jnp.int32, (256, 256), 0)
    col_at = lax.broadcasted_iota(jnp.int32, (256, 256), 1)
    from_head = (row_at >> 2) & 15
    source = ((from_head & 1) * 8 + (from_head >> 1)) * 16 + (row_at >> 6) * 4 + (row_at & 3)
    picks = jnp.where(col_at == source, 1.0, 0.0).astype(jnp.bfloat16)
    arrived(2, q_all.at[0:256, :])
    mixed = [
        jnp.concatenate([q_all[i + group * 128 : i + group * 128 + 128, :] for i in (0, 256)], axis=0)
        for group in range(2)
    ]
    picked = dot(picks, jnp.concatenate(mixed, axis=1)).astype(jnp.bfloat16)
    for group in range(2):
        for part in range(4):
            q_rows[group * ROWS : group * ROWS + ROWS, part * 384 : part * 384 + 384] = picked[
                part * ROWS : part * ROWS + ROWS, group * 384 : group * 384 + 384
            ]

    lane = lax.broadcasted_iota(jnp.int32, (ROWS, 128), 1)
    wide = lax.broadcasted_iota(jnp.int32, (2 * ROWS, 128), 1)

    def project():
        q_full[...] = dot(q_rows[...], v_uq[...]).astype(jnp.bfloat16).astype(jnp.float32)

    def absorb_all():
        cosine = jnp.concatenate([table_ref[0:8, :]] * 16, axis=0)
        sine = jnp.concatenate([table_ref[8:16, :]] * 16, axis=0)

        def absorb(h, nope, pe):
            turned = jnp.where(wide < 32, pltpu.roll(pe, 96, 1), pltpu.roll(pe, 32, 1))
            rotated = pe * cosine + turned * sine
            first = rotated.astype(jnp.bfloat16)
            second = pltpu.roll(rotated, 64, 1).astype(jnp.bfloat16)
            absorbed = dot(nope.astype(jnp.bfloat16), v_uk[h]).astype(jnp.bfloat16)
            for group in range(2):
                rows = pl.ds(group * GROUP + h * ROWS, ROWS)
                part = slice(group * ROWS, group * ROWS + ROWS)
                queries[rows, 0:128] = first[part]
                queries[rows, 640:768] = second[part]
                queries[rows, 128:640] = absorbed[part]

        for two in range(HEADS // 2):
            at = two * 384
            middle = q_full[:, at + 128 : at + 256]
            end = pltpu.roll(q_full[:, at + 256 : at + 384], 64, 1)
            absorb(2 * two, q_full[:, at : at + 128], middle)
            absorb(2 * two + 1, jnp.where(wide < 64, pltpu.roll(middle, 64, 1), end), end)

    def score(rows, units, with_draft=False):
        low = [jnp.concatenate([keys[u * UNIT + t] for u in units], axis=0) for t in range(4)]
        high = [jnp.concatenate([keys[u * UNIT + 4 + t] for u in units], axis=0) for t in range(4)]
        rope = jnp.concatenate([keys[u * UNIT + 8] for u in units], axis=0)
        left = dot_t(queries[rows, 0:640], jnp.concatenate([rope] + low, axis=1))
        right = dot_t(queries[rows, 128:768], jnp.concatenate(high + [rope], axis=1))
        values = [jnp.concatenate(low, axis=1), jnp.concatenate(high, axis=1)]
        scores = [left * SCALE, right * SCALE]
        if with_draft:
            bias = jnp.concatenate([draft_bias[...]] * (BLOCK // ROWS), axis=0)
            scores.append(dot_t(queries[rows, 0:640], draft[...]) * SCALE + bias)
            values.append(draft[:, 128:640])
        return jnp.concatenate(scores, axis=1), jnp.concatenate(values, axis=0)

    def update(rows, scores, values, first=False):
        peak = jnp.max(scores, axis=1, keepdims=True)
        if first:
            new_top = jnp.broadcast_to(peak, (BLOCK, 128))
        else:
            old_top = top[rows, :]
            new_top = jnp.maximum(old_top, peak)
            factor = jnp.exp2(old_top - new_top)
        e = jnp.exp2(scores - new_top[:, 0:1])
        part = jnp.sum(e, axis=1, keepdims=True)
        summed = dot(e.astype(jnp.bfloat16), values)
        if first:
            total[rows, :] = jnp.broadcast_to(part, (BLOCK, 128))
            acc[rows, :] = summed
        else:
            total[rows, :] = total[rows, :] * factor + part
            acc[rows, :] = acc[rows, :] * factor[:, 0:1] + summed
        top[rows, :] = new_top

    held = []

    def settle():
        if held:
            update(*held.pop())

    def attend(items):
        for group, block, units, first, with_draft in items:
            rows = pl.ds(group * GROUP + block * BLOCK, BLOCK)
            now = (rows, *score(rows, units, with_draft), first)
            settle()
            held.append(now)

    def gather_draft():
        draft[ROWS:128, :] = jnp.zeros((128 - ROWS, 640), jnp.bfloat16)
        chosen = dot(picks, d_all[...]).astype(jnp.bfloat16)
        draft[0:ROWS, 0:128] = chosen[0:ROWS, 128:256]
        for part in range(4):
            draft[0:ROWS, 128 + part * 128 : 256 + part * 128] = chosen[part * ROWS : part * ROWS + ROWS, 0:128]
        row = lax.broadcasted_iota(jnp.int32, (ROWS, 128), 0)
        col = lax.broadcasted_iota(jnp.int32, (ROWS, 128), 1)
        begin = jnp.zeros((ROWS, 128), jnp.int32)
        for i in range(8):
            begin = jnp.where((col >> 3) == i, start_ref[i], begin)
        seen = ((row >> 3) == (col >> 3)) & (col <= row) & (begin <= (col & 7))
        draft_bias[...] = jnp.where(seen, 0.0, -1e30)

    def context(group, h):
        rows = pl.ds(group * GROUP + h * ROWS, ROWS)
        ctx = (acc[rows, :] * (1.0 / total[rows, 0:1])).astype(jnp.bfloat16)
        return dot(ctx, v_uv[h]), top[rows, :] + jnp.log2(total[rows, :])

    def pair(group, units, first=False, with_draft=False):
        return [(group, block, units, first, with_draft) for block in range(2)]

    weights[0].wait()
    weights[1].wait()
    project()
    streams[1].arrive_a()
    absorb_all()
    streams[0].arrive_side(0)
    streams[1].arrive_side(0)
    attend(pair(1, chunk((0, 1), (0,)), True))
    streams[2].arrive_a()
    arrived(1, d_all.at[0:112, :])
    send(d_all.at[d_half, :], d_all.at[d_half, :], sibling, 4, 3)
    own_early = pair(0, chunk((0, 1), (0,)), True)
    attend(own_early[:1])
    streams[3].arrive_a()
    streams[0].arrive_b()
    attend(own_early[1:])
    arrived(3, d_all.at[0:128, :])
    gather_draft()
    streams[2].arrive_side(0)
    streams[3].arrive_side(0)
    attend(pair(1, chunk((2, 3), (0,))))
    streams[1].arrive_b()
    attend(pair(0, chunk((2, 3), (0,))))
    streams[2].arrive_b()
    streams[0].arrive_side(1)
    streams[1].arrive_side(1)
    peer_middle = pair(1, chunk((0, 1), (1, 2)))
    attend(peer_middle[:1])
    streams[3].arrive_b()
    attend(peer_middle[1:])
    attend(pair(0, chunk((0, 1), (1, 2))))
    streams[0].arrive_far()
    streams[1].arrive_far()
    streams[2].arrive_side(1)
    streams[3].arrive_side(1)
    attend(pair(1, chunk((2, 3), (1, 2))))
    streams[2].arrive_far()
    streams[3].arrive_far()
    streams[0].arrive_side(3)
    streams[1].arrive_side(3)
    attend(pair(1, chunk((0, 1), (3,))))
    streams[2].arrive_side(3)
    streams[3].arrive_side(3)
    weights[2].wait()
    def hand_over(part):
        if part == 0:
            shares[...] = jnp.zeros((128, 128), jnp.float32)
        for i in range(HEADS // 2):
            h = part * (HEADS // 2) + i
            value, share = context(1, h)
            o_send[part, :, i * VD : i * VD + VD] = value.astype(jnp.bfloat16)
            shares[0:ROWS, :] = jnp.where(lane == h, share, shares[0:ROWS, :])
        send(o_send.at[part], o_recv.at[part], partner, 5, 4)
        if part:
            s_send[...] = jnp.transpose(shares[...])[0:HEADS, :]
            send(s_send, s_recv, partner, 6, 5)

    attend(pair(1, chunk((2, 3), (3,))))
    hand_over(0)
    rest = pair(0, chunk((2, 3), (1, 2)), False, True) + pair(0, chunk((0, 1, 2, 3), (3,)))
    settle()
    hand_over(1)
    attend(rest)
    settle()
    own = []

    def finish():
        own.extend(context(0, h) for h in range(HEADS))

    def collect():
        arrived(4, o_recv)
        arrived(5, s_recv)

    def merge():
        shares[0:HEADS, :] = s_recv[...]
        others = jnp.transpose(shares[...])
        for h, (value, share) in enumerate(own):
            other = jnp.broadcast_to(others[0:ROWS, h : h + 1], (ROWS, 128))
            mine = 1.0 / (1.0 + jnp.exp2(jnp.minimum(other - share, 120.0)))
            theirs = 1.0 / (1.0 + jnp.exp2(jnp.minimum(share - other, 120.0)))
            part, at = h // 4, (h % 4) * VD
            peer = o_recv[part, :, at : at + VD].astype(jnp.float32)
            out_ref[:, h * VD : h * VD + VD] = (value * mine + peer * theirs).astype(jnp.bfloat16)

    def drain():
        gone(0, tiles(0, 127))
        gone(1, q_all.at[0:240, :])
        gone(2, d_all.at[0:112, :])
        gone(3, q_all.at[0:256, :])
        gone(4, d_all.at[0:128, :])
        gone(5, o_send)
        gone(6, s_send)

    finish()
    collect()
    merge()
    drain()


def on_device(
    q_latent, draft_latent, draft_rope, draft_start, prompt_latent, prompt_rope, w_uq, w_uk, w_uv
):
    vmem = pl.BlockSpec(memory_space=pltpu.VMEM)
    hbm = pl.BlockSpec(memory_space=pltpu.HBM)
    bf16, f32 = jnp.bfloat16, jnp.float32
    return pl.pallas_call(
        kernel,
        name="attention",
        out_shape=jax.ShapeDtypeStruct((ROWS, HEADS * VD), bf16),
        in_specs=[hbm] * 10,
        out_specs=vmem,
        scratch_shapes=[
            pltpu.VMEM((4, QLORA), bf16),
            pltpu.VMEM((4, KVL), bf16),
            pltpu.VMEM((4, ROPE), bf16),
            pltpu.SMEM((8,), jnp.int32),
            pltpu.VMEM((32, KVL), bf16),
            pltpu.VMEM((32, ROPE), bf16),
            pltpu.VMEM((16, 128), f32),
            pltpu.VMEM((UNITS * UNIT, 16, 128), bf16),
            pltpu.VMEM((16, 384), bf16),
            pltpu.VMEM((512, 384), bf16),
            pltpu.VMEM((16, 256), bf16),
            pltpu.VMEM((256, 256), bf16),
            pltpu.VMEM((16, 640), f32),
            pltpu.VMEM((2 * ROWS, QLORA), bf16),
            pltpu.VMEM((2 * ROWS, QLORA), f32),
            pltpu.VMEM((2 * GROUP, 768), bf16),
            pltpu.VMEM((128, 640), bf16),
            pltpu.VMEM((ROWS, 128), f32),
            pltpu.VMEM((2 * GROUP, KVL), f32),
            pltpu.VMEM((2 * GROUP, 128), f32),
            pltpu.VMEM((2 * GROUP, 128), f32),
            pltpu.VMEM((2, ROWS, HEADS * VD // 2), bf16),
            pltpu.VMEM((2, ROWS, HEADS * VD // 2), bf16),
            pltpu.VMEM((HEADS, 128), f32),
            pltpu.VMEM((HEADS, 128), f32),
            pltpu.VMEM((128, 128), f32),
            pltpu.VMEM((QLORA, HEADS * (NOPE + ROPE)), bf16),
            pltpu.VMEM((HEADS, NOPE, KVL), bf16),
            pltpu.VMEM((HEADS, KVL, VD), bf16),
            pltpu.SemaphoreType.DMA((10,)),
            pltpu.SemaphoreType.DMA((7,)),
            pltpu.SemaphoreType.DMA((36,)),
        ],
        compiler_params=pltpu.CompilerParams(
            collective_id=0, has_side_effects=True, vmem_limit_bytes=64 * 2**20
        ),
    )(
        q_latent, draft_latent, draft_rope, draft_start, prompt_latent, prompt_rope,
        rotation_table(), w_uq, w_uk, w_uv,
    )


def solution(mesh):
    in_specs = (
        P(("grp", "head"), None),
        P(("grp", "head"), None),
        P(("grp", "head"), None),
        P("grp"),
        P(("grp", "head"), None),
        P(("grp", "head"), None),
        P(None, "head"),
        P("head", None, None),
        P("head", None, None),
    )
    out_specs = P("grp", "head")
    return jax.shard_map(
        on_device, mesh=mesh, in_specs=in_specs, out_specs=out_specs, check_vma=False
    )
```

```python
import math

import jax
import jax.numpy as jnp
import numpy as np
from jax import lax
from jax.experimental import pallas as pl
from jax.experimental.pallas import tpu as pltpu
from jax.sharding import PartitionSpec as P

MESH = pl.DeviceIdType.MESH
KVL = 512
ROPE = 64
NOPE = 128
VD = 128
DRAFT = 8
PROMPT = 8192
QLORA = 1536
ROWS = 64
HEADS = 8
GROUP = ROWS * HEADS
SCALE = math.log2(math.e) / math.sqrt(NOPE + ROPE)
UNIT = 9
UNITS = 128
BLOCK = 256
NT = (((1,), (1,)), ((), ()))


def rotation_table():
    half = ROPE // 2
    freq = np.float32(10000.0) ** (-np.arange(half, dtype=np.float32) / np.float32(half))
    position = PROMPT + np.arange(DRAFT, dtype=np.float32)
    angle = (position[:, None] * freq[None, :].astype(np.float32)).astype(np.float64)
    zero = np.zeros((DRAFT, 2 * half))
    cosine = np.concatenate([np.cos(angle), np.cos(angle), zero], axis=1)
    sine = np.concatenate([-np.sin(angle), np.sin(angle), zero], axis=1)
    return np.concatenate([cosine, sine], axis=0).astype(np.float32)


def unit(stream, bs, cs, as_):
    return ((stream * 4 + bs) * 2 + cs) * 4 + as_


def chunk(streams, bss):
    return [unit(s, b, c, a) for s in streams for b in bss for c in (0, 1) for a in range(4)]


def dot_t(a, b):
    return lax.dot_general(a, b, NT, preferred_element_type=jnp.float32)


def dot(a, b):
    return jnp.dot(a, b, preferred_element_type=jnp.float32)


def kernel(
    ql_in, dl_in, dr_in, start_in, pl_in, pr_in, table_in, w_uq, w_uk, w_uv, out_ref,
    ql_ref, dl_ref, dr_ref, start_ref, pl_ref, pr_ref, table_ref,
    keys, q_send, q_all, d_send, d_all, q_stage, q_rows, q_full, queries, draft, draft_bias, acc, top, total,
    o_send, o_recv, s_send, s_recv, shares, v_uq, v_uk, v_uv, local_sem, send_sem, recv_sem,
):
    grp, head = lax.axis_index("grp"), lax.axis_index("head")
    x, y, z, core = head // 4, (grp // 8) * 2 + (head // 2) % 2, grp % 8, head % 2
    toward = 2 * (z % 2) - 1

    def place(px, py, pz, pc):
        return ((py // 2) * 8 + pz, px * 4 + (py % 2) * 2 + pc)

    def at_a(step):
        return place((x + step * core + 4) % 4, (y + step * (1 - core) + 4) % 4, z, core)

    def at_b(step):
        return place((x + step * (1 - core) + 4) % 4, (y + step * core + 4) % 4, z, core)

    def at_z(step):
        return place(x, y, (z + step + 8) % 8, core)

    beside = y + 1 - 2 * (y % 2)
    sibling = place(x, y, z, 1 - core)
    partner = at_z(-toward)
    beyond = (z - toward + 8) % 8
    near = [place((x + dx) % 4, y, z, core) for dx in (1, 3, 2)]
    near += [place((x + dx) % 4, beside, z, core) for dx in (0, 1, 3, 2)]
    across = [place((x + dx) % 4, py, beyond, core) for py in (y, beside) for dx in (0, 1, 3, 2)]
    greeted = near + across + [place(x, (y + 3 + 2 * (y % 2)) % 4, z, core), place(x, (y + 2) % 4, z, core)]
    greeted += [at_z(toward), at_z(3 * toward), at_z(2), at_z(-2), sibling]

    barrier = pltpu.get_barrier_semaphore()
    for device in greeted:
        pl.semaphore_signal(barrier, inc=1, device_id=device, device_id_type=MESH)
    loads = [
        pltpu.make_async_copy(src, dst, local_sem.at[i])
        for i, (src, dst) in enumerate((
            (pl_in, pl_ref), (pr_in, pr_ref), (ql_in, ql_ref), (dl_in, dl_ref), (dr_in, dr_ref),
            (table_in, table_ref), (start_in, start_ref), (w_uq, v_uq), (w_uk, v_uk), (w_uv, v_uv),
        ))
    ]
    inputs, weights = loads[:7], loads[7:]
    for copy in inputs:
        copy.start()
    for copy in weights:
        copy.start()
    for copy in inputs:
        copy.wait()

    def send(src, dst, device, left, landed):
        pltpu.make_async_remote_copy(
            src_ref=src, dst_ref=dst, send_sem=send_sem.at[left], recv_sem=recv_sem.at[landed],
            device_id=device, device_id_type=MESH,
        ).start()

    def arrived(landed, ref):
        pltpu.make_async_copy(ref, ref, recv_sem.at[landed]).wait()

    def gone(left, ref):
        pltpu.make_async_copy(ref, ref, send_sem.at[left]).wait()

    def tiles(at, count=1, first=0, last=0):
        return keys.at[pl.ds(at * UNIT + first, count * UNIT - first - last)]

    def move(src, dst, count, device, landed, first=0, last=0):
        send(tiles(src, count, first, last), tiles(dst, count, first, last), device, 0, landed)

    for row in range(2):
        for lane in range(4):
            keys[row * 4 + lane] = pl_ref[row * 16 : row * 16 + 16, lane * 128 : lane * 128 + 128]
    keys[8] = jnp.concatenate([pr_ref[0:16, :], pr_ref[16:32, :]], axis=1)
    q_stage[...] = jnp.zeros(q_stage.shape, jnp.float32)
    for part in range(4):
        q_stage[part * 4 : part * 4 + 4, 0:384] = ql_ref[:, part * 384 : part * 384 + 384].astype(jnp.float32)
        q_stage[part * 4 : part * 4 + 4, 384:512] = dl_ref[:, part * 128 : part * 128 + 128].astype(jnp.float32)
    q_stage[0:4, 512:576] = dr_ref[...].astype(jnp.float32)
    q_send[...] = q_stage[:, 0:384].astype(jnp.bfloat16)
    d_send[...] = q_stage[:, 384:640].astype(jnp.bfloat16)

    def slot(base):
        return pl.ds(pl.multiple_of(base + head // 2 * 16, 16), 16)

    q_all[slot(core * 256), :] = q_send[...]
    d_all[slot(core * 128), :] = d_send[...]

    pl.semaphore_wait(barrier, len(greeted))

    for device in near:
        send(q_send, q_all.at[slot(core * 256), :], device, 1, 0)
    for device in across:
        send(q_send, q_all.at[slot(core * 256 + 128), :], device, 1, 0)
    for stream, step in ((1, toward), (2, -2 * toward), (3, 3 * toward)):
        move(unit(0, 0, 0, 0), unit(stream, 0, 0, 0), 1, at_z(step), 8 + stream)

    class Stream:
        def __init__(self, index):
            self.index = index
            self.sem = 12 + index * 6

        def spread(self, k):
            own = unit(self.index, 0, 0, k)
            move(own, unit(self.index, 1, 0, k), 1, at_b(1), self.sem + 1)
            move(own, unit(self.index, 2, 0, k), 1, at_b(-1), self.sem + 1)

        def to_sibling(self, bs, count=1):
            sem = self.sem + 3 + (bs + 1) // 2
            for i in range(bs, bs + count):
                move(unit(self.index, i, 0, 0), unit(self.index, i, 1, 0), 4, sibling, sem)

        def start(self):
            if self.index:
                arrived(8 + self.index, tiles(0))
            for k, step in ((1, 1), (2, -1), (3, 2)):
                move(unit(self.index, 0, 0, 0), unit(self.index, 0, 0, k), 1, at_a(step), self.sem)
            self.spread(0)

        def arrive_a(self):
            arrived(self.sem, tiles(0, 3))
            for k in (1, 2, 3):
                self.spread(k)
            self.to_sibling(0)

        def arrive_b(self):
            cut = UNIT // 2
            arrived(self.sem + 1, tiles(0, 8))
            for k in range(4):
                here = unit(self.index, 3, 0, k)
                move(unit(self.index, 1, 0, k), here, 1, at_b(1), self.sem + 2, 0, UNIT - cut)
                move(unit(self.index, 2, 0, k), here, 1, at_b(-1), self.sem + 2, cut, 0)
            self.to_sibling(1, 2)

        def arrive_far(self):
            arrived(self.sem + 2, tiles(0, 4))
            self.to_sibling(3)

        def arrive_side(self, bs):
            arrived(self.sem + 3 + (bs + 1) // 2, tiles(0, 8 if bs == 1 else 4))

    streams = [Stream(i) for i in range(4)]
    streams[0].start()
    streams[1].start()
    for device in near:
        send(d_send, d_all.at[slot(core * 128), :], device, 2, 1)
    streams[0].arrive_a()
    arrived(0, q_all.at[0:240, :])
    q_half = pl.ds(pl.multiple_of(core * 256, 256), 256)
    send(q_all.at[q_half, :], q_all.at[q_half, :], sibling, 3, 2)
    streams[2].start()
    streams[3].start()
    d_half = pl.ds(pl.multiple_of(core * 128, 128), 128)

    row_at = lax.broadcasted_iota(jnp.int32, (256, 256), 0)
    col_at = lax.broadcasted_iota(jnp.int32, (256, 256), 1)
    from_head = (row_at >> 2) & 15
    source = ((from_head & 1) * 8 + (from_head >> 1)) * 16 + (row_at >> 6) * 4 + (row_at & 3)
    picks = jnp.where(col_at == source, 1.0, 0.0).astype(jnp.bfloat16)
    arrived(2, q_all.at[0:256, :])
    mixed = [
        jnp.concatenate([q_all[i + group * 128 : i + group * 128 + 128, :] for i in (0, 256)], axis=0)
        for group in range(2)
    ]
    picked = dot(picks, jnp.concatenate(mixed, axis=1)).astype(jnp.bfloat16)
    for group in range(2):
        for part in range(4):
            q_rows[group * ROWS : group * ROWS + ROWS, part * 384 : part * 384 + 384] = picked[
                part * ROWS : part * ROWS + ROWS, group * 384 : group * 384 + 384
            ]

    lane = lax.broadcasted_iota(jnp.int32, (ROWS, 128), 1)
    wide = lax.broadcasted_iota(jnp.int32, (2 * ROWS, 128), 1)

    def project():
        q_full[...] = dot(q_rows[...], v_uq[...]).astype(jnp.bfloat16).astype(jnp.float32)

    def absorb_all():
        cosine = jnp.concatenate([table_ref[0:8, :]] * 16, axis=0)
        sine = jnp.concatenate([table_ref[8:16, :]] * 16, axis=0)

        def absorb(h, nope, pe):
            turned = jnp.where(wide < 32, pltpu.roll(pe, 96, 1), pltpu.roll(pe, 32, 1))
            rotated = pe * cosine + turned * sine
            first = rotated.astype(jnp.bfloat16)
            second = pltpu.roll(rotated, 64, 1).astype(jnp.bfloat16)
            absorbed = dot(nope.astype(jnp.bfloat16), v_uk[h]).astype(jnp.bfloat16)
            for group in range(2):
                rows = pl.ds(group * GROUP + h * ROWS, ROWS)
                part = slice(group * ROWS, group * ROWS + ROWS)
                queries[rows, 0:128] = first[part]
                queries[rows, 640:768] = second[part]
                queries[rows, 128:640] = absorbed[part]

        for two in range(HEADS // 2):
            at = two * 384
            middle = q_full[:, at + 128 : at + 256]
            end = pltpu.roll(q_full[:, at + 256 : at + 384], 64, 1)
            absorb(2 * two, q_full[:, at : at + 128], middle)
            absorb(2 * two + 1, jnp.where(wide < 64, pltpu.roll(middle, 64, 1), end), end)

    def score(rows, units, with_draft=False):
        low = [jnp.concatenate([keys[u * UNIT + t] for u in units], axis=0) for t in range(4)]
        high = [jnp.concatenate([keys[u * UNIT + 4 + t] for u in units], axis=0) for t in range(4)]
        rope = jnp.concatenate([keys[u * UNIT + 8] for u in units], axis=0)
        left = dot_t(queries[rows, 0:640], jnp.concatenate([rope] + low, axis=1))
        right = dot_t(queries[rows, 128:768], jnp.concatenate(high + [rope], axis=1))
        values = [jnp.concatenate(low, axis=1), jnp.concatenate(high, axis=1)]
        scores = [left * SCALE, right * SCALE]
        if with_draft:
            bias = jnp.concatenate([draft_bias[...]] * (BLOCK // ROWS), axis=0)
            scores.append(dot_t(queries[rows, 0:640], draft[...]) * SCALE + bias)
            values.append(draft[:, 128:640])
        return jnp.concatenate(scores, axis=1), jnp.concatenate(values, axis=0)

    def update(rows, scores, values, first=False):
        peak = jnp.max(scores, axis=1, keepdims=True)
        if first:
            new_top = jnp.broadcast_to(peak, (BLOCK, 128))
        else:
            old_top = top[rows, :]
            new_top = jnp.maximum(old_top, peak)
            factor = jnp.exp2(old_top - new_top)
        e = jnp.exp2(scores - new_top[:, 0:1])
        part = jnp.sum(e, axis=1, keepdims=True)
        summed = dot(e.astype(jnp.bfloat16), values)
        if first:
            total[rows, :] = jnp.broadcast_to(part, (BLOCK, 128))
            acc[rows, :] = summed
        else:
            total[rows, :] = total[rows, :] * factor + part
            acc[rows, :] = acc[rows, :] * factor[:, 0:1] + summed
        top[rows, :] = new_top

    held = []

    def settle():
        if held:
            update(*held.pop())

    def attend(items):
        for group, block, units, first, with_draft in items:
            rows = pl.ds(group * GROUP + block * BLOCK, BLOCK)
            now = (rows, *score(rows, units, with_draft), first)
            settle()
            held.append(now)

    def gather_draft():
        draft[ROWS:128, :] = jnp.zeros((128 - ROWS, 640), jnp.bfloat16)
        chosen = dot(picks, d_all[...]).astype(jnp.bfloat16)
        draft[0:ROWS, 0:128] = chosen[0:ROWS, 128:256]
        for part in range(4):
            draft[0:ROWS, 128 + part * 128 : 256 + part * 128] = chosen[part * ROWS : part * ROWS + ROWS, 0:128]
        row = lax.broadcasted_iota(jnp.int32, (ROWS, 128), 0)
        col = lax.broadcasted_iota(jnp.int32, (ROWS, 128), 1)
        begin = jnp.zeros((ROWS, 128), jnp.int32)
        for i in range(8):
            begin = jnp.where((col >> 3) == i, start_ref[i], begin)
        seen = ((row >> 3) == (col >> 3)) & (col <= row) & (begin <= (col & 7))
        draft_bias[...] = jnp.where(seen, 0.0, -1e30)

    def context(group, h):
        rows = pl.ds(group * GROUP + h * ROWS, ROWS)
        ctx = (acc[rows, :] * (1.0 / total[rows, 0:1])).astype(jnp.bfloat16)
        return dot(ctx, v_uv[h]), top[rows, :] + jnp.log2(total[rows, :])

    def pair(group, units, first=False, with_draft=False):
        return [(group, block, units, first, with_draft) for block in range(2)]

    weights[0].wait()
    weights[1].wait()
    project()
    streams[1].arrive_a()
    absorb_all()
    streams[0].arrive_side(0)
    streams[1].arrive_side(0)
    attend(pair(1, chunk((0, 1), (0,)), True))
    streams[2].arrive_a()
    arrived(1, d_all.at[0:112, :])
    send(d_all.at[d_half, :], d_all.at[d_half, :], sibling, 4, 3)
    own_early = pair(0, chunk((0, 1), (0,)), True)
    attend(own_early[:1])
    streams[3].arrive_a()
    streams[0].arrive_b()
    attend(own_early[1:])
    arrived(3, d_all.at[0:128, :])
    gather_draft()
    streams[2].arrive_side(0)
    streams[3].arrive_side(0)
    attend(pair(1, chunk((2, 3), (0,))))
    streams[1].arrive_b()
    attend(pair(0, chunk((2, 3), (0,))))
    streams[2].arrive_b()
    streams[0].arrive_side(1)
    streams[1].arrive_side(1)
    peer_middle = pair(1, chunk((0, 1), (1, 2)))
    attend(peer_middle[:1])
    streams[3].arrive_b()
    attend(peer_middle[1:])
    attend(pair(0, chunk((0, 1), (1, 2))))
    streams[0].arrive_far()
    streams[1].arrive_far()
    streams[2].arrive_side(1)
    streams[3].arrive_side(1)
    peer_late = pair(1, chunk((2, 3), (1, 2)))
    attend(peer_late[:1])
    streams[2].arrive_far()
    attend(peer_late[1:])
    streams[3].arrive_far()
    streams[0].arrive_side(3)
    streams[1].arrive_side(3)
    attend(pair(1, chunk((0, 1), (3,))))
    streams[2].arrive_side(3)
    streams[3].arrive_side(3)
    weights[2].wait()
    def hand_over(part):
        if part == 0:
            shares[...] = jnp.zeros((128, 128), jnp.float32)
        for i in range(HEADS // 2):
            h = part * (HEADS // 2) + i
            value, share = context(1, h)
            o_send[part, :, i * VD : i * VD + VD] = value.astype(jnp.bfloat16)
            shares[0:ROWS, :] = jnp.where(lane == h, share, shares[0:ROWS, :])
        send(o_send.at[part], o_recv.at[part], partner, 5, 4)
        if part:
            s_send[...] = jnp.transpose(shares[...])[0:HEADS, :]
            send(s_send, s_recv, partner, 6, 5)

    attend(pair(1, chunk((2, 3), (3,))))
    hand_over(0)
    rest = pair(0, chunk((2, 3), (1, 2)), False, True) + pair(0, chunk((0, 1, 2, 3), (3,)))
    settle()
    hand_over(1)
    attend(rest)
    settle()
    own = []

    def finish():
        own.extend(context(0, h) for h in range(HEADS))

    def collect():
        arrived(4, o_recv)
        arrived(5, s_recv)

    def merge():
        shares[0:HEADS, :] = s_recv[...]
        others = jnp.transpose(shares[...])
        for h, (value, share) in enumerate(own):
            other = jnp.broadcast_to(others[0:ROWS, h : h + 1], (ROWS, 128))
            mine = 1.0 / (1.0 + jnp.exp2(jnp.minimum(other - share, 120.0)))
            theirs = 1.0 / (1.0 + jnp.exp2(jnp.minimum(share - other, 120.0)))
            part, at = h // 4, (h % 4) * VD
            peer = o_recv[part, :, at : at + VD].astype(jnp.float32)
            out_ref[:, h * VD : h * VD + VD] = (value * mine + peer * theirs).astype(jnp.bfloat16)

    def drain():
        gone(0, tiles(0, 127))
        gone(1, q_all.at[0:240, :])
        gone(2, d_all.at[0:112, :])
        gone(3, q_all.at[0:256, :])
        gone(4, d_all.at[0:128, :])
        gone(5, o_send)
        gone(6, s_send)

    finish()
    collect()
    merge()
    drain()


def on_device(
    q_latent, draft_latent, draft_rope, draft_start, prompt_latent, prompt_rope, w_uq, w_uk, w_uv
):
    vmem = pl.BlockSpec(memory_space=pltpu.VMEM)
    hbm = pl.BlockSpec(memory_space=pltpu.HBM)
    bf16, f32 = jnp.bfloat16, jnp.float32
    return pl.pallas_call(
        kernel,
        name="attention",
        out_shape=jax.ShapeDtypeStruct((ROWS, HEADS * VD), bf16),
        in_specs=[hbm] * 10,
        out_specs=vmem,
        scratch_shapes=[
            pltpu.VMEM((4, QLORA), bf16),
            pltpu.VMEM((4, KVL), bf16),
            pltpu.VMEM((4, ROPE), bf16),
            pltpu.SMEM((8,), jnp.int32),
            pltpu.VMEM((32, KVL), bf16),
            pltpu.VMEM((32, ROPE), bf16),
            pltpu.VMEM((16, 128), f32),
            pltpu.VMEM((UNITS * UNIT, 16, 128), bf16),
            pltpu.VMEM((16, 384), bf16),
            pltpu.VMEM((512, 384), bf16),
            pltpu.VMEM((16, 256), bf16),
            pltpu.VMEM((256, 256), bf16),
            pltpu.VMEM((16, 640), f32),
            pltpu.VMEM((2 * ROWS, QLORA), bf16),
            pltpu.VMEM((2 * ROWS, QLORA), f32),
            pltpu.VMEM((2 * GROUP, 768), bf16),
            pltpu.VMEM((128, 640), bf16),
            pltpu.VMEM((ROWS, 128), f32),
            pltpu.VMEM((2 * GROUP, KVL), f32),
            pltpu.VMEM((2 * GROUP, 128), f32),
            pltpu.VMEM((2 * GROUP, 128), f32),
            pltpu.VMEM((2, ROWS, HEADS * VD // 2), bf16),
            pltpu.VMEM((2, ROWS, HEADS * VD // 2), bf16),
            pltpu.VMEM((HEADS, 128), f32),
            pltpu.VMEM((HEADS, 128), f32),
            pltpu.VMEM((128, 128), f32),
            pltpu.VMEM((QLORA, HEADS * (NOPE + ROPE)), bf16),
            pltpu.VMEM((HEADS, NOPE, KVL), bf16),
            pltpu.VMEM((HEADS, KVL, VD), bf16),
            pltpu.SemaphoreType.DMA((10,)),
            pltpu.SemaphoreType.DMA((7,)),
            pltpu.SemaphoreType.DMA((36,)),
        ],
        compiler_params=pltpu.CompilerParams(
            collective_id=0, has_side_effects=True, vmem_limit_bytes=64 * 2**20
        ),
    )(
        q_latent, draft_latent, draft_rope, draft_start, prompt_latent, prompt_rope,
        rotation_table(), w_uq, w_uk, w_uv,
    )


def solution(mesh):
    in_specs = (
        P(("grp", "head"), None),
        P(("grp", "head"), None),
        P(("grp", "head"), None),
        P("grp"),
        P(("grp", "head"), None),
        P(("grp", "head"), None),
        P(None, "head"),
        P("head", None, None),
        P("head", None, None),
    )
    out_specs = P("grp", "head")
    return jax.shard_map(
        on_device, mesh=mesh, in_specs=in_specs, out_specs=out_specs, check_vma=False
    )
```
